32 devices in a mesh: seq: 8 (over z, x), head: 4 (over y, core).
Axes of the slice: x: 2, y: 2, z: 4, core: 2. Of those that a mesh axis runs over, the one named last changes fastest.
Arguments:
- latent: float32 [2048, 128], P('seq'), may hold values from -6 to 6
- w_in: bfloat16 [128, 3072], replicated, may hold values from -0.5 to 0.5
- w_query: bfloat16 [3072, 3072], P(None, 'head'), may hold values from -0.109375 to 0.109375
- w_key: bfloat16 [3072, 3072], P(None, 'head'), may hold values from -0.109375 to 0.109375
- w_value: bfloat16 [3072, 3072], P(None, 'head'), may hold values from -0.109375 to 0.109375
- w_attn_out: bfloat16 [3072, 3072], P('head'), may hold values from -0.109375 to 0.109375
- w_up: bfloat16 [3072, 12288], P('seq', 'head'), may hold values from -0.109375 to 0.109375
- w_down: bfloat16 [12288, 3072], P('head', 'seq'), may hold values from -0.0546875 to 0.0546875
- w_final: bfloat16 [3072, 256], replicated, may hold values from -0.109375 to 0.109375
- gain_attn: float32 [3072], replicated, may hold values from 0.5 to 1.5
- gain_mlp: float32 [3072], replicated, may hold values from 0.5 to 1.5
- gain_final: float32 [3072], replicated, may hold values from 0.5 to 1.5
Outputs:
- restored: float32 [2048, 128], P('seq')
The draws below stay inside these ranges and needn't reach their ends.
All inputs are finite; a program needn't handle non-finite values.
Results may differ from the reference program's by a relative error of at most 0.013.
Values may be sent and summed in bfloat16 or wider, within the bound.
No kernel may reach another device: no remote copies, remote signals or barrier semaphores. Data moves between devices by JAX's collectives and lax.ppermute only.
A program may use at most 192 MiB of HBM per device.

```python
import jax
import jax.numpy as jnp
from jax import lax

D = 3072
HEADS = 24
HEAD_DIM = 128
FF = 12288
C = 128
ITERS = 2
LENGTH = 2048
N_HEAD = 4


def shard_levels(own_key, dims, pieces, low, top_value):
    level, own = 1.0, jax.random.fold_in(own_key, 6)
    for dim, parts in pieces:
        draws = jnp.exp(jax.random.uniform(jax.random.fold_in(own, dim), (parts,), jnp.float32, low / len(pieces), top_value / len(pieces)))
        level = level * jnp.repeat(draws, dims[dim] // parts).reshape([-1 if axis == dim else 1 for axis in range(len(dims))])
    return level


def bell_draw(stream_key, shape, deviation, limit, shards=(), dtype=jnp.bfloat16):
    result = jax.random.normal(stream_key, shape, jnp.float32) * deviation
    if len(shards) > 0:
        result = shard_levels(stream_key, shape, shards, -0.22, 0.18) * result
    return jnp.clip(result, min=-limit, max=limit).astype(dtype)


def setup_inputs(seed: int = 0) -> dict:
    seeds = jax.random.split(jax.random.key(seed), 13)
    latent = bell_draw(seeds[0], (LENGTH, C), 1.0, 6.0, ((0, 8),), jnp.float32)
    w_in = bell_draw(seeds[1], (C, D), C ** -0.5, 0.5)
    w_query = bell_draw(seeds[2], (D, HEADS * HEAD_DIM), D ** -0.5, 0.109375, ((1, 4),))
    w_key = bell_draw(seeds[3], (D, HEADS * HEAD_DIM), D ** -0.5, 0.109375, ((1, 4),))
    w_value = bell_draw(seeds[4], (D, HEADS * HEAD_DIM), D ** -0.5, 0.109375, ((1, 4),))
    w_attn_out = bell_draw(seeds[5], (HEADS * HEAD_DIM, D), (HEADS * HEAD_DIM) ** -0.5, 0.109375, ((0, 4),))
    w_up = bell_draw(seeds[6], (D, FF), D ** -0.5, 0.109375, ((0, 8), (1, 4)))
    w_down = bell_draw(seeds[7], (FF, D), FF ** -0.5, 0.0546875, ((0, 4), (1, 8)))
    w_final = bell_draw(seeds[8], (D, 2 * C), D ** -0.5, 0.109375)
    gain_attn = jnp.clip(1.0 + 0.1 * jax.random.normal(seeds[9], (D,), jnp.float32), 0.5, 1.5)
    gain_mlp = jnp.clip(1.0 + 0.1 * jax.random.normal(seeds[10], (D,), jnp.float32), 0.5, 1.5)
    gain_final = jnp.clip(1.0 + 0.1 * jax.random.normal(seeds[11], (D,), jnp.float32), 0.5, 1.5)
    return dict(latent=latent, w_in=w_in, w_query=w_query, w_key=w_key, w_value=w_value, w_attn_out=w_attn_out, w_up=w_up, w_down=w_down, w_final=w_final, gain_attn=gain_attn, gain_mlp=gain_mlp, gain_final=gain_final)


EPSILON = 1e-05

def layer_norm(stream, gain):
    center = stream - lax.optimization_barrier(jnp.mean(stream, axis=-1, keepdims=True))
    spread = lax.optimization_barrier(jnp.mean(center * center, axis=-1, keepdims=True))
    return center * lax.rsqrt(spread + EPSILON) * gain

def sinusoid(positions, model_width):
    pair_count = model_width // 2
    frequency = jnp.exp(-jnp.log(10000.0) * 2.0 * jnp.arange(pair_count).astype(jnp.float32) / model_width)
    angles = positions[:, None] * frequency[None, :]
    return jnp.concatenate([jnp.sin(angles), jnp.cos(angles)], axis=1)

def causal_attention(queries, key_rows, value_rows):
    length = queries.shape[0]
    query_heads = queries.astype(jnp.float32).reshape(length, HEADS, HEAD_DIM).transpose(1, 0, 2)
    key_heads = key_rows.astype(jnp.float32).reshape(length, HEADS, HEAD_DIM).transpose(1, 0, 2)
    value_heads = value_rows.reshape(length, HEADS, HEAD_DIM).transpose(1, 0, 2)
    visible = jnp.arange(length)[None, :] <= jnp.arange(length)[:, None]

    def one_head(operands):
        query_head, key_head, value_head = operands
        scores = jnp.dot(query_head, key_head.T, precision=lax.Precision.HIGHEST)
        weights_now = jnp.where(visible, jnp.exp(jnp.where(visible, scores, 0.0)), 0.0)
        totals = lax.optimization_barrier(jnp.sum(weights_now, axis=-1, keepdims=True))
        probs = weights_now.astype(jnp.bfloat16)
        return jnp.dot(probs, value_head, preferred_element_type=jnp.float32) / totals
    outputs = lax.map(one_head, (query_heads, key_heads, value_heads))
    return outputs.transpose(1, 0, 2).reshape(length, HEADS * HEAD_DIM).astype(jnp.bfloat16)

def grouped_sum(left, right):
    group_width = left.shape[1] // N_HEAD
    total = jnp.zeros((left.shape[0], right.shape[1]), jnp.float32)
    for group_index in range(N_HEAD):
        lower = group_index * group_width
        upper = lower + group_width
        partial_term = jnp.dot(left[:, lower:upper], right[lower:upper], preferred_element_type=jnp.float32)
        total = total + lax.optimization_barrier(partial_term.astype(jnp.bfloat16)).astype(jnp.float32)
    return total

def reference(latent, w_in, w_query, w_key, w_value, w_attn_out, w_up, w_down, w_final, gain_attn, gain_mlp, gain_final):
    length = latent.shape[0]
    positions = jnp.arange(length).astype(jnp.float32)
    embedding = sinusoid(positions, D)
    current = latent
    for step_index in range(ITERS):
        stream_in = jnp.dot(current.astype(jnp.bfloat16), w_in, preferred_element_type=jnp.float32) + embedding
        normed = layer_norm(stream_in, gain_attn).astype(jnp.bfloat16)
        queries = (jnp.dot(normed, w_query, preferred_element_type=jnp.float32) * HEAD_DIM ** (-0.5)).astype(jnp.bfloat16)
        key_rows = jnp.dot(normed, w_key, preferred_element_type=jnp.float32).astype(jnp.bfloat16)
        value_rows = jnp.dot(normed, w_value, preferred_element_type=jnp.float32).astype(jnp.bfloat16)
        attended = causal_attention(queries, key_rows, value_rows)
        stream_attn = stream_in + grouped_sum(attended, w_attn_out)
        normed_mlp = layer_norm(stream_attn, gain_mlp).astype(jnp.bfloat16)
        hidden = jax.nn.gelu(jnp.dot(normed_mlp, w_up, preferred_element_type=jnp.float32), approximate=True).astype(jnp.bfloat16)
        stream_mlp = stream_attn + grouped_sum(hidden, w_down)
        final_normed = layer_norm(stream_mlp, gain_final).astype(jnp.bfloat16)
        params_out = jnp.dot(final_normed, w_final, preferred_element_type=jnp.float32)
        shifted = jnp.concatenate([jnp.zeros((1, params_out.shape[1]), jnp.float32), params_out[:-1]], axis=0)
        current = latent * jnp.exp(jnp.tanh(shifted[:, C:])) + shifted[:, :C]
    return current[::-1]
```

```python
import functools

import jax
import jax.numpy as jnp
from jax import lax
from jax.experimental import pallas as pl
from jax.experimental.pallas import tpu as pltpu
from jax.sharding import PartitionSpec as P

HEAD_DIM = 128
ITERS = 2
EPSILON = 1e-05
FINE = 64
BF16, F32 = jnp.bfloat16, jnp.float32


def layer_norm(stream, gain):
    center = stream - jnp.mean(stream, axis=-1, keepdims=True)
    spread = jnp.mean(center * center, axis=-1, keepdims=True)
    return center * lax.rsqrt(spread + EPSILON) * gain


class Grid:
    def __init__(self):
        self.ns, self.nh = lax.axis_size("seq"), lax.axis_size("head")
        self.s, self.h = lax.axis_index("seq"), lax.axis_index("head")
        self.outer, self.groups = self.ns // 2, self.nh // 2
        self.z, self.x = self.s // 2, self.s % 2
        self.y, self.c = self.h // 2, self.h % 2
        self.ring = []
        for y in range(self.groups):
            line = [(z, y) for z in range(self.outer)]
            self.ring += line if y % 2 == 0 else line[::-1]
        self.place = {zy: i for i, zy in enumerate(self.ring)}

    def move(self, value, target):
        route = []
        for s in range(self.ns):
            for h in range(self.nh):
                there = target(s, h)
                if there is not None:
                    route.append((s * self.nh + h, there[0] * self.nh + there[1]))
        return lax.ppermute(value, ("seq", "head"), route)

    def ring_step(self, value, step):
        def target(s, h):
            i = self.place[(s // 2, h // 2)]
            z, y = self.ring[(i + step) % len(self.ring)]
            return z * 2 + s % 2, y * 2 + h % 2

        return self.move(value, target)

    def seq_shift(self, value, step):
        return self.move(value, lambda s, h: ((s + step) % self.ns, h))

    def outer_shift(self, value, step):
        return self.move(value, lambda s, h: ((s + 2 * step) % self.ns, h))

    def pair_swap(self, value):
        return self.move(value, lambda s, h: (s ^ 1, h))

    def group_shift(self, value, step):
        return self.move(value, lambda s, h: (s, (h + 2 * step) % self.nh))

    def core_swap(self, value):
        return self.move(value, lambda s, h: (s, h ^ 1))


def in_order(parts, mine):
    count = len(parts)
    twice = jnp.stack(parts + parts[:-1])
    return lax.dynamic_slice_in_dim(twice, (count - mine) % count, count, axis=0)


def gather_rows(grid, own):
    over_seq = [own] + [grid.seq_shift(own, -j) for j in range(1, grid.ns)]
    by_seq = in_order(over_seq, grid.s)
    over_group = [by_seq] + [grid.group_shift(by_seq, -j) for j in range(1, grid.groups)]
    by_group = in_order(over_group, grid.y)
    other = grid.core_swap(by_group)
    by_core = jnp.where(grid.c == 0, jnp.stack([by_group, other]), jnp.stack([other, by_group]))
    return by_core.transpose(2, 1, 0, 3, 4).reshape(-1, own.shape[-1])


def gather_ring(grid, own):
    size = len(grid.ring)
    half, cut = size // 2, own.shape[0] // 2
    pieces = {0: own}
    ahead = back = own
    for j in range(1, half):
        ahead, back = grid.ring_step(ahead, 1), grid.ring_step(back, -1)
        pieces[-j], pieces[j] = ahead, back
    pieces[half] = jnp.concatenate(
        [grid.ring_step(ahead[:cut], 1), grid.ring_step(back[cut:], -1)], axis=0
    )
    return pieces


def reduce_ring(grid, terms):
    size = len(grid.ring)
    half, cut = size // 2, terms[0].shape[0] // 2
    ahead = grid.ring_step(terms[half][:cut], 1)
    back = grid.ring_step(terms[half][cut:], -1)
    for j in range(half - 1, 0, -1):
        if j == half - 1:
            up, down = terms[j].astype(F32), terms[-j].astype(F32)
            up = jnp.concatenate([up[:cut] + ahead.astype(F32), up[cut:]], axis=0)
            down = jnp.concatenate([down[:cut], down[cut:] + back.astype(F32)], axis=0)
        else:
            up = terms[j].astype(F32) + ahead.astype(F32)
            down = terms[-j].astype(F32) + back.astype(F32)
        ahead, back = grid.ring_step(up.astype(BF16), 1), grid.ring_step(down.astype(BF16), -1)
    return terms[0].astype(F32) + ahead.astype(F32) + back.astype(F32)


def reduce_head(grid, term):
    rows, width = term.shape
    blocks = term.reshape(grid.groups, 2, rows // grid.nh, width)
    keep = lax.dynamic_index_in_dim(blocks, grid.c, 1, keepdims=False)
    give = lax.dynamic_index_in_dim(blocks, 1 - grid.c, 1, keepdims=False)
    both = keep.astype(F32) + grid.core_swap(give).astype(F32)
    total = lax.dynamic_index_in_dim(both, grid.y, 0, keepdims=False)
    rounded = both.astype(BF16)
    for j in range(1, grid.groups):
        send = lax.dynamic_index_in_dim(rounded, (grid.y + j) % grid.groups, 0, keepdims=False)
        total = total + grid.group_shift(send, j).astype(F32)
    return total


def spread_weights(grid, w_up, w_down):
    rows, hidden = w_up.shape
    chunk = hidden // grid.outer
    outer, ns = grid.outer, grid.ns
    up_parts, down_parts = [], []
    for kind in range(2):
        for j in range(outer):
            to = (grid.z + j) % outer
            if kind == 0:
                part = lax.dynamic_slice_in_dim(w_up, to * chunk, chunk, axis=1)
            else:
                part = lax.dynamic_slice_in_dim(w_down, to * chunk, chunk, axis=0)
            if j:
                part = grid.outer_shift(part, j)
            other = grid.pair_swap(part)
            source = (grid.z - j) % outer
            (up_parts, down_parts)[kind].append((source * 2 + grid.x, part))
            (up_parts, down_parts)[kind].append((source * 2 + 1 - grid.x, other))
    up = jnp.zeros((rows * ns, chunk), w_up.dtype)
    down = jnp.zeros((chunk, rows * ns), w_down.dtype)
    for place, part in up_parts:
        up = lax.dynamic_update_slice_in_dim(up, part, place * rows, axis=0)
    for place, part in down_parts:
        down = lax.dynamic_update_slice_in_dim(down, part, place * rows, axis=1)
    return up, down


def angle_tables(tokens, width):
    pairs = width // 2
    frequency = jnp.exp(-jnp.log(10000.0) * 2.0 * jnp.arange(pairs).astype(F32) / width)
    coarse = (jnp.arange(tokens // FINE) * FINE).astype(F32)[:, None] * frequency[None, :]
    fine = jnp.arange(FINE).astype(F32)[:, None] * frequency[None, :]
    return jnp.sin(coarse), jnp.cos(coarse), jnp.sin(fine), jnp.cos(fine)


def embed(sin_a, cos_a, sin_b, cos_b):
    return jnp.concatenate([sin_a * cos_b + cos_a * sin_b, cos_a * cos_b - sin_a * sin_b], axis=-1)


def project_kernel(
    scales, cur_ref, w_in_ref, sin_a, cos_a, sin_b, cos_b, gain_ref, *rest
):
    count = len(scales)
    weights, outs, normed = rest[:count], rest[count : 2 * count], rest[2 * count]
    for part in range(cur_ref.shape[0] // FINE):
        rows = pl.ds(part * FINE, FINE)
        stream = jnp.dot(cur_ref[rows, :], w_in_ref[...], preferred_element_type=F32)
        stream = stream + embed(
            sin_a[pl.ds(part, 1), :], cos_a[pl.ds(part, 1), :], sin_b[...], cos_b[...]
        )
        normed[rows, :] = layer_norm(stream, gain_ref[...]).astype(BF16)
    for scale, weight, out in zip(scales, weights, outs):
        value = jnp.dot(normed[...], weight[...], preferred_element_type=F32)
        out[...] = (value * scale if scale != 1.0 else value).astype(BF16)


def project(current, w_in, tables, gain, weights, scales, block):
    tokens, channels = current.shape
    width = w_in.shape[1]
    sin_a, cos_a, sin_b, cos_b = tables
    coarse = block // FINE
    sin_a, cos_a = (t.reshape(tokens // block, coarse, width // 2) for t in (sin_a, cos_a))
    whole = lambda shape: pl.BlockSpec(shape, lambda i: (0,) * len(shape))
    in_specs = [
        pl.BlockSpec((block, channels), lambda i: (i, 0)),
        whole(w_in.shape),
        pl.BlockSpec((None, coarse, width // 2), lambda i: (i, 0, 0)),
        pl.BlockSpec((None, coarse, width // 2), lambda i: (i, 0, 0)),
        whole(sin_b.shape),
        whole(cos_b.shape),
        whole((1, width)),
    ] + [whole(w.shape) for w in weights]
    macs = tokens * width * (channels + sum(w.shape[1] for w in weights))
    return pl.pallas_call(
        functools.partial(project_kernel, scales),
        grid=(tokens // block,),
        in_specs=in_specs,
        out_specs=[pl.BlockSpec((block, w.shape[1]), lambda i: (i, 0)) for w in weights],
        out_shape=[jax.ShapeDtypeStruct((tokens, w.shape[1]), BF16) for w in weights],
        scratch_shapes=[pltpu.VMEM((block, width), BF16)],
        compiler_params=pltpu.CompilerParams(vmem_limit_bytes=56 * 2**20),
        cost_estimate=pl.CostEstimate(
            flops=2 * macs, bytes_accessed=2 * sum(w.size for w in weights), transcendentals=0
        ),
        name="project",
    )(current, w_in, sin_a, cos_a, sin_b, cos_b, gain.reshape(1, width), *weights)


def attend_kernel(block, index_ref, q_ref, k_ref, v_ref, out_ref):
    own = index_ref[0]
    queries = q_ref[...]
    rows = queries.shape[0]

    def visit(j, state, masked):
        totals, weighted = state
        here = pl.ds(pl.multiple_of(j * block, block), block)
        scores = lax.dot_general(
            queries, k_ref[here, :], (((1,), (1,)), ((), ())), preferred_element_type=F32
        )
        if masked:
            query = lax.broadcasted_iota(jnp.int32, scores.shape, 0)
            key = lax.broadcasted_iota(jnp.int32, scores.shape, 1)
            seen = key <= query
            weights = jnp.where(seen, jnp.exp(jnp.where(seen, scores, 0.0)), 0.0)
        else:
            weights = jnp.exp(scores)
        totals = totals + jnp.sum(weights, axis=-1, keepdims=True)
        weighted = weighted + jnp.dot(
            weights.astype(BF16), v_ref[here, :], preferred_element_type=F32
        )
        return totals, weighted

    state = (jnp.zeros((rows, 1), F32), jnp.zeros((rows, v_ref.shape[1]), F32))
    state = lax.fori_loop(0, own, lambda j, st: visit(j, st, False), state)
    totals, weighted = visit(own, state, True)
    out_ref[...] = (weighted / totals).astype(BF16)


def attend(index, queries, keys, values):
    rows, columns = queries.shape
    tokens = keys.shape[0]
    whole = pl.BlockSpec((tokens, HEAD_DIM), lambda i, n: (0, i))
    own = pl.BlockSpec((rows, HEAD_DIM), lambda i, n: (0, i))
    return pl.pallas_call(
        functools.partial(attend_kernel, rows),
        grid_spec=pltpu.PrefetchScalarGridSpec(
            num_scalar_prefetch=1,
            grid=(columns // HEAD_DIM,),
            in_specs=[own, whole, whole],
            out_specs=own,
        ),
        out_shape=jax.ShapeDtypeStruct((rows, columns), BF16),
        compiler_params=pltpu.CompilerParams(vmem_limit_bytes=32 * 2**20),
        cost_estimate=pl.CostEstimate(
            flops=4 * rows * tokens * columns,
            bytes_accessed=4 * tokens * columns,
            transcendentals=rows * tokens * columns // HEAD_DIM,
        ),
        name="attend",
    )(index.reshape(1).astype(jnp.int32), queries, keys, values)


def per_device(
    latent, w_in, w_query, w_key, w_value, w_attn_out, w_up, w_down, w_final,
    gain_attn, gain_mlp, gain_final,
):
    grid = Grid()
    rows, channels = latent.shape
    width = w_in.shape[1]
    sub = rows // grid.nh
    tokens = rows * grid.ns
    tables = angle_tables(tokens, width)
    start = grid.s * rows + grid.h * sub

    latent_own = lax.dynamic_slice_in_dim(latent, grid.h * sub, sub)
    next_row = grid.seq_shift(latent[:1], -1)
    latent_next = lax.dynamic_slice_in_dim(
        jnp.concatenate([latent, next_row]), grid.h * sub + 1, sub
    )
    latent_all = gather_rows(grid, latent_own.astype(BF16))
    up, down = spread_weights(grid, w_up, w_down)

    current = latent_all
    for step_index in range(ITERS):
        keys, values = project(
            current, w_in, tables, gain_attn, (w_key, w_value), (1.0, 1.0), min(256, rows)
        )
        block_rows = lax.dynamic_slice_in_dim(current, grid.s * rows, rows)
        coarse = rows // FINE
        own_tables = tuple(
            lax.dynamic_slice_in_dim(t, grid.s * coarse, coarse) for t in tables[:2]
        ) + tables[2:]
        (queries,) = project(
            block_rows, w_in, own_tables, gain_attn, (w_query,), (HEAD_DIM**-0.5,), rows
        )
        attended = attend(grid.s, queries, keys, values)
        own_rows = lax.dynamic_slice_in_dim(current, start, sub)
        position = (start + jnp.arange(sub)) // FINE
        offset = (start + jnp.arange(sub)) % FINE
        stream_in = jnp.dot(own_rows, w_in, preferred_element_type=F32) + embed(
            *(jnp.take(t, position, axis=0) for t in tables[:2]),
            *(jnp.take(t, offset, axis=0) for t in tables[2:]),
        )
        stream_attn = stream_in + reduce_head(
            grid, jnp.dot(attended, w_attn_out, preferred_element_type=F32).astype(BF16)
        )
        pieces = gather_ring(grid, layer_norm(stream_attn, gain_mlp).astype(BF16))
        order = sorted(pieces)
        mine = jnp.concatenate([pieces[k] for k in order])
        others = jnp.concatenate([grid.core_swap(pieces[k]) for k in order])
        both = jnp.concatenate([mine, others])
        hidden = jax.nn.gelu(
            jnp.dot(both, up, preferred_element_type=F32), approximate=True
        ).astype(BF16)
        terms = jnp.dot(hidden, down, preferred_element_type=F32).astype(BF16)
        from_core = grid.core_swap(terms[mine.shape[0] :])
        summed = (terms[: mine.shape[0]].astype(F32) + from_core.astype(F32)).astype(BF16)
        by_offset = {k: summed[i * sub : (i + 1) * sub] for i, k in enumerate(order)}
        stream_mlp = stream_attn + reduce_ring(grid, by_offset)
        final = layer_norm(stream_mlp, gain_final).astype(BF16)
        params = jnp.dot(final, w_final, preferred_element_type=F32)
        moved = latent_next * jnp.exp(jnp.tanh(params[:, channels:])) + params[:, :channels]
        if step_index < ITERS - 1:
            gathered = gather_rows(grid, moved.astype(BF16))
            current = jnp.concatenate([latent_all[:1], gathered[:-1]])

    mirrored = grid.move(moved, lambda s, h: (grid.ns - 1 - s, h))

    def after(s, h):
        place = s * grid.nh + h + 1
        if place == grid.ns * grid.nh:
            return None
        return grid.ns - 1 - place // grid.nh, place % grid.nh

    first = grid.move(moved[-1:], after)
    is_start = (grid.s == grid.ns - 1) & (grid.h == 0)
    first = jnp.where(is_start, latent_all[:1].astype(F32), first)
    block = jnp.concatenate([first, mirrored[:-1]])
    over_group = [block] + [grid.group_shift(block, -j) for j in range(1, grid.groups)]
    by_group = in_order(over_group, grid.y)
    other = grid.core_swap(by_group)
    by_core = jnp.where(
        grid.c == 0, jnp.stack([by_group, other], 1), jnp.stack([other, by_group], 1)
    )
    return by_core.reshape(rows, channels)[::-1]


def solution(mesh):
    in_specs = (
        P("seq", None),
        P(),
        P(None, "head"),
        P(None, "head"),
        P(None, "head"),
        P("head", None),
        P("seq", "head"),
        P("head", "seq"),
        P(),
        P(),
        P(),
        P(),
    )
    return jax.shard_map(
        per_device, mesh=mesh, in_specs=in_specs, out_specs=P("seq", None), check_vma=False
    )
```

```python
import functools

import jax
import jax.numpy as jnp
from jax import lax
from jax.experimental import pallas as pl
from jax.experimental.pallas import tpu as pltpu
from jax.sharding import PartitionSpec as P

HEAD_DIM = 128
ITERS = 2
EPSILON = 1e-05
FINE = 64
BLOCKS = 2
STRIP = 256
CHUNK = 1024
HEADS_A_STEP = 2
BF16, F32 = jnp.bfloat16, jnp.float32


def layer_norm(stream, gain):
    center = stream - jnp.mean(stream, axis=-1, keepdims=True)
    spread = jnp.mean(center * center, axis=-1, keepdims=True)
    return center * lax.rsqrt(spread + EPSILON) * gain


class Grid:
    def __init__(self):
        self.ns, self.nh = lax.axis_size("seq"), lax.axis_size("head")
        self.s, self.h = lax.axis_index("seq"), lax.axis_index("head")
        self.outer, self.groups = self.ns // 2, self.nh // 2
        self.z, self.x = self.s // 2, self.s % 2
        self.y, self.c = self.h // 2, self.h % 2
        self.ring = []
        for y in range(self.groups):
            line = [(z, y) for z in range(self.outer)]
            self.ring += line if y % 2 == 0 else line[::-1]
        self.place = {zy: i for i, zy in enumerate(self.ring)}

    def move(self, value, target):
        route = []
        for s in range(self.ns):
            for h in range(self.nh):
                there = target(s, h)
                if there is not None:
                    route.append((s * self.nh + h, there[0] * self.nh + there[1]))
        return lax.ppermute(value, ("seq", "head"), route)

    def ring_step(self, value, step):
        def target(s, h):
            i = self.place[(s // 2, h // 2)]
            z, y = self.ring[(i + step) % len(self.ring)]
            return z * 2 + s % 2, y * 2 + h % 2

        return self.move(value, target)

    def seq_shift(self, value, step):
        return self.move(value, lambda s, h: ((s + step) % self.ns, h))

    def outer_shift(self, value, step):
        return self.move(value, lambda s, h: ((s + 2 * step) % self.ns, h))

    def pair_swap(self, value):
        return self.move(value, lambda s, h: (s ^ 1, h))

    def group_shift(self, value, step):
        return self.move(value, lambda s, h: (s, (h + 2 * step) % self.nh))

    def core_swap(self, value):
        return self.move(value, lambda s, h: (s, h ^ 1))


def after_kernel(value_ref, *refs):
    refs[-1][0] = value_ref[0]


def after(value, arrays):
    smem = pl.BlockSpec(memory_space=pltpu.SMEM)
    made = pl.pallas_call(
        after_kernel,
        in_specs=[smem] + [pl.BlockSpec(memory_space=pl.ANY)] * len(arrays),
        out_specs=smem,
        out_shape=jax.ShapeDtypeStruct((1,), jnp.int32),
        name="after",
    )(value.reshape(1).astype(jnp.int32), *arrays)
    return made[0]


def place_kernel(count, sub, shifted, dest_ref, *refs):
    parts, out = refs[:count], refs[count + shifted]
    wide = refs[-1] if shifted else out
    n = 0
    for part in parts:
        for first in range(0, part.shape[0], sub):
            there = pl.ds(pl.multiple_of(dest_ref[n] * sub, sub), sub)
            wide[there, :] = part[pl.ds(first, sub), :].astype(wide.dtype)
            n += 1
    if shifted:
        moved = pltpu.roll(wide[...], 1, axis=0)
        top = lax.broadcasted_iota(jnp.int32, moved.shape, 0) == 0
        out[...] = jnp.where(top, refs[count][:1, :].astype(F32), moved).astype(out.dtype)


def place(parts, dests, sub, first=None):
    width, total = parts[0].shape[1], sum(p.shape[0] for p in parts)
    vmem = pl.BlockSpec(memory_space=pltpu.VMEM)
    extra = [] if first is None else [first]
    return pl.pallas_call(
        functools.partial(place_kernel, len(parts), sub, len(extra)),
        in_specs=[pl.BlockSpec(memory_space=pltpu.SMEM)] + [vmem] * (len(parts) + len(extra)),
        out_specs=vmem,
        out_shape=jax.ShapeDtypeStruct((total, width), parts[0].dtype),
        scratch_shapes=[pltpu.VMEM((total, width), F32)] if extra else [],
        name="place",
    )(jnp.stack(dests).astype(jnp.int32), *parts, *extra)


def gather_rows(grid, own, first=None, gates=(), late_gates=()):
    sub = own.shape[0]
    over_seq = [own] + [grid.seq_shift(own, -j) for j in range(1, grid.ns)]
    turn = after(grid.s, gates) if gates else grid.s
    line = place(over_seq, [(turn + j) % grid.ns for j in range(grid.ns)], sub)
    lines = [line] + [grid.group_shift(line, -j) for j in range(1, grid.groups)]
    heads = [((grid.y + j) % grid.groups) * 2 + grid.c for j in range(grid.groups)]
    lines += [grid.core_swap(line) for line in lines]
    heads += [head ^ 1 for head in heads]
    zero = after(grid.s, late_gates) - grid.s if late_gates else 0
    dests = [zero + seq * grid.nh + head for head in heads for seq in range(grid.ns)]
    return place(lines, dests, sub, first)


def gather_ring(grid, own, zero):
    size = len(grid.ring)
    half, cut = size // 2, own.shape[0] // 2
    pieces = {0: own}
    ahead = back = own
    for j in range(1, half):
        ahead, back = grid.ring_step(ahead, 1), grid.ring_step(back, -1)
        pieces[-j], pieces[j] = ahead, back
    pieces[half] = jnp.concatenate(
        [
            grid.ring_step(lax.dynamic_slice_in_dim(ahead, zero, cut), 1),
            grid.ring_step(lax.dynamic_slice_in_dim(back, zero + cut, cut), -1),
        ],
        axis=0,
    )
    return pieces


def reduce_ring(grid, terms):
    size = len(grid.ring)
    half, cut = size // 2, terms[0].shape[0] // 2
    ahead = grid.ring_step(terms[half][:cut].astype(BF16), 1)
    back = grid.ring_step(terms[half][cut:].astype(BF16), -1)
    for j in range(half - 1, 0, -1):
        up, down = terms[j], terms[-j]
        if j == half - 1:
            up = jnp.concatenate([up[:cut] + ahead.astype(F32), up[cut:]], axis=0)
            down = jnp.concatenate([down[:cut], down[cut:] + back.astype(F32)], axis=0)
        else:
            up, down = up + ahead.astype(F32), down + back.astype(F32)
        ahead, back = grid.ring_step(up.astype(BF16), 1), grid.ring_step(down.astype(BF16), -1)
    return terms[0] + ahead.astype(F32) + back.astype(F32)


def reduce_head(grid, term, zero):
    rows, width = term.shape
    blocks = term.reshape(grid.groups, 2, rows // grid.nh, width)
    keep = lax.dynamic_index_in_dim(blocks, grid.c + zero, 1, keepdims=False)
    give = lax.dynamic_index_in_dim(blocks, 1 - grid.c + zero, 1, keepdims=False)
    both = keep.astype(F32) + grid.core_swap(give).astype(F32)
    total = lax.dynamic_index_in_dim(both, grid.y, 0, keepdims=False)
    rounded = both.astype(BF16)
    for j in range(1, grid.groups):
        send = lax.dynamic_index_in_dim(rounded, (grid.y + j) % grid.groups, 0, keepdims=False)
        total = total + grid.group_shift(send, j).astype(F32)
    return total


class Weights:
    def __init__(self, grid, w_up, w_down):
        self.grid, self.sources = grid, (w_up, w_down)
        self.chunk, self.rows = w_up.shape[1] // grid.outer, w_up.shape[0]
        steps = [(kind, j) for kind in range(2) for j in range(1, grid.outer)]
        size, longer = divmod(len(steps), 4)
        self.phases = []
        for i in range(4):
            count = size + (i < longer)
            self.phases.append(steps[:count])
            steps = steps[count:]
        self.arrived, self.swapped = {}, {}
        for kind in range(2):
            self.arrived[kind, 0] = self.cut(kind, grid.z, 0)
            self.swapped[kind, 0] = grid.pair_swap(self.arrived[kind, 0])

    def partner(self, z, j):
        outer = self.grid.outer
        return z ^ j if outer & (outer - 1) == 0 else (2 * outer + j - z) % outer if j else z

    def cut(self, kind, to, zero):
        return lax.dynamic_slice_in_dim(
            self.sources[kind], to * self.chunk + zero, self.chunk, axis=1 - kind
        )

    def send(self, phase, zero):
        grid = self.grid
        for kind, j in self.phases[phase]:
            part = self.cut(kind, self.partner(grid.z, j), zero)
            self.arrived[kind, j] = grid.move(
                part, lambda s, h, j=j: (self.partner(s // 2, j) * 2 + s % 2, h)
            )
        return [self.arrived[step] for step in self.phases[phase]]

    def swap(self, phase):
        for step in self.phases[phase]:
            self.swapped[step] = self.grid.pair_swap(self.arrived[step])
        return [self.swapped[step] for step in self.phases[phase]]

    def parts(self):
        grid, places, made = self.grid, [], ([], [])
        for j in range(grid.outer):
            at = self.partner(grid.z, j) * 2
            places += [at + grid.x, at + 1 - grid.x]
            for kind in range(2):
                made[kind].extend([self.arrived[kind, j], self.swapped[kind, j]])
        if self.rows % 128:
            for kind in range(2):
                shape = [self.rows * grid.ns] * 2
                shape[1 - kind] = self.chunk
                full = jnp.zeros(shape, BF16)
                for at, part in zip(places, made[kind]):
                    full = lax.dynamic_update_slice_in_dim(full, part, at * self.rows, axis=kind)
                made[kind][:] = [full]
            places = [jnp.zeros_like(grid.s)]
        return jnp.stack(places).astype(jnp.int32), *made


def angle_tables(tokens, width):
    pairs = width // 2
    frequency = jnp.exp(-jnp.log(10000.0) * 2.0 * jnp.arange(pairs).astype(F32) / width)
    coarse = (jnp.arange(tokens // FINE) * FINE).astype(F32)[:, None] * frequency[None, :]
    fine = jnp.arange(FINE).astype(F32)[:, None] * frequency[None, :]
    return jnp.sin(coarse), jnp.cos(coarse), jnp.sin(fine), jnp.cos(fine)


def embedding_means(sin_a, cos_a, sin_b, cos_b):
    left = jnp.concatenate([sin_a, cos_a], axis=1)
    right = jnp.concatenate([cos_b - sin_b, cos_b + sin_b], axis=1)
    total = jnp.dot(left, right.T, precision=lax.Precision.HIGHEST)
    return (total / left.shape[1]).reshape(-1, 1)


def embed(sin_a, cos_a, sin_b, cos_b):
    return jnp.concatenate([sin_a * cos_b + cos_a * sin_b, cos_a * cos_b - sin_a * sin_b], axis=-1)


def embed_kernel(blocks, with_query, ids_ref, *refs):
    w_in_ref, gain_ref, mean_ref, sin_a, cos_a, sin_b, cos_b, wk_ref, wv_ref = refs[:9]
    refs = refs[9:]
    if with_query:
        wq_ref, ek_ref, ev_ref, cross_ref, eq_ref, aq_ref, scaled, plain = refs
    else:
        ek_ref, ev_ref, cross_ref, ak_ref, av_ref, scaled, plain = refs
    step = pl.program_id(0)
    w_in = w_in_ref[...]

    @pl.when(step == 0)
    def _():
        wide = w_in.astype(F32)
        center = wide - jnp.mean(wide, axis=-1, keepdims=True)
        center = (center * gain_ref[...]).astype(BF16)
        pairs = [(wq_ref, aq_ref)] if with_query else [(wk_ref, ak_ref), (wv_ref, av_ref)]
        for weight, out in pairs:
            out[...] = jnp.dot(center, weight[...], preferred_element_type=F32).astype(BF16)

    pairs = sin_b.shape[1]
    for column in range(0, pairs, STRIP):
        low, high = pl.ds(column, STRIP), pl.ds(pairs + column, STRIP)
        for part in range(scaled.shape[0] // FINE):
            sin_coarse, cos_coarse = sin_a[pl.ds(part, 1), low], cos_a[pl.ds(part, 1), low]
            for fine in range(0, FINE, 16):
                rows, thin = pl.ds(part * FINE + fine, 16), pl.ds(fine, 16)
                sin_fine, cos_fine, mean = sin_b[thin, low], cos_b[thin, low], mean_ref[rows, :]
                sines = sin_coarse * cos_fine + cos_coarse * sin_fine - mean
                cosines = cos_coarse * cos_fine - sin_coarse * sin_fine - mean
                scaled[rows, low] = (sines * gain_ref[:, low]).astype(BF16)
                scaled[rows, high] = (cosines * gain_ref[:, high]).astype(BF16)
                plain[rows, low] = sines.astype(BF16)
                plain[rows, high] = cosines.astype(BF16)

    @pl.when(step < blocks)
    def _():
        cross_ref[...] = lax.dot_general(
            plain[...], w_in, (((1,), (1,)), ((), ())), preferred_element_type=F32
        )
        ek_ref[...] = jnp.dot(scaled[...], wk_ref[...], preferred_element_type=F32).astype(BF16)
        ev_ref[...] = jnp.dot(scaled[...], wv_ref[...], preferred_element_type=F32).astype(BF16)

    if with_query:

        @pl.when(step == blocks)
        def _():
            rows = eq_ref.shape[0]
            first = pl.multiple_of(ids_ref[blocks + 1] * rows, rows)
            own = scaled[pl.ds(first, rows), :]
            eq_ref[...] = jnp.dot(own, wq_ref[...], preferred_element_type=F32).astype(BF16)


def embed_products(index, part, rows, w_in, tables, mean, gain, weights):
    sin_a, cos_a, sin_b, cos_b = tables
    channels, width = w_in.shape
    columns = weights[0].shape[1]
    tokens = sin_a.shape[0] * FINE
    block = rows * BLOCKS if tokens % (2 * rows * BLOCKS) == 0 else rows
    coarse, count = block // FINE, tokens // block // 2
    with_query = len(weights) == 3
    sin_a, cos_a = (t.reshape(2 * count, coarse, width // 2) for t in (sin_a, cos_a))
    ids = [part * count + i for i in range(count)]
    ids += [index // (block // rows), index % (block // rows)]
    ids = jnp.stack([jnp.asarray(i, jnp.int32) for i in ids])

    def whole(shape):
        return pl.BlockSpec(
            shape, lambda i, ids: (0,) * len(shape), pipeline_mode=pl.Buffered(buffer_count=1)
        )

    fixed = lambda shape: pl.BlockSpec(shape, lambda i, ids: (0, 0))
    coarse_spec = pl.BlockSpec((None, coarse, width // 2), lambda i, ids: (ids[i], 0, 0))
    token_in = pl.BlockSpec((block, 1), lambda i, ids: (ids[i], 0))
    token = lambda n: pl.BlockSpec((block, n), lambda i, ids: (jnp.minimum(i, count - 1), 0))
    struct = jax.ShapeDtypeStruct
    half = tokens // 2
    small = struct((channels, columns), BF16)
    return pl.pallas_call(
        functools.partial(embed_kernel, count, with_query),
        grid_spec=pltpu.PrefetchScalarGridSpec(
            num_scalar_prefetch=1,
            grid=(count + with_query,),
            in_specs=[
                whole(w_in.shape),
                whole((1, width)),
                token_in,
                coarse_spec,
                coarse_spec,
                whole(sin_b.shape),
                whole(cos_b.shape),
            ]
            + [whole(w.shape) for w in weights],
            out_specs=[token(columns), token(columns), token(channels)]
            + [fixed((rows if with_query else channels, columns)), fixed((channels, columns))],
            scratch_shapes=[pltpu.VMEM((block, width), BF16), pltpu.VMEM((block, width), BF16)],
        ),
        out_shape=[
            struct((half, columns), BF16),
            struct((half, columns), BF16),
            struct((half, channels), F32),
            struct((rows, columns), BF16) if with_query else small,
            small,
        ],
        compiler_params=pltpu.CompilerParams(vmem_limit_bytes=60 * 2**20),
        cost_estimate=pl.CostEstimate(flops=1, bytes_accessed=1, transcendentals=0),
        name="embed_products",
    )(ids, w_in, gain.reshape(1, width), mean, sin_a, cos_a, sin_b, cos_b, *weights)


def attend_kernel(
    width, scale, chunk, index_ref, cur_ref, gram_ref, size_ref, eq_ref, aq_ref, ak_ref, av_ref,
    ek_one, ek_two, ev_one, ev_two, cross_one, cross_two, out_ref, inverse,
):
    own = index_ref[0]
    rows, tokens = eq_ref.shape[0], cur_ref.shape[0]
    channels = cur_ref.shape[1]

    def of(refs, first):
        ref, start = refs[first >= tokens // 2], first % (tokens // 2)
        return ref.at[pl.ds(start, chunk)]

    ek_refs, ev_refs, cross_refs = (ek_one, ek_two), (ev_one, ev_two), (cross_one, cross_two)

    @pl.when(pl.program_id(0) == 0)
    def _():
        for first in range(0, tokens, chunk):
            here = pl.ds(first, chunk)
            both = jnp.dot(cur_ref[here, :], gram_ref[...], preferred_element_type=F32)
            both = both[:, :channels] + both[:, channels:] + 2.0 * of(cross_refs, first)[...]
            spread = jnp.sum(both * cur_ref[here, :].astype(F32), axis=-1, keepdims=True)
            inverse[here, :] = jnp.broadcast_to(
                lax.rsqrt(spread / width + size_ref[here, :] + EPSILON), (chunk, HEAD_DIM)
            )

    mine = pl.ds(pl.multiple_of(own * rows, rows), rows)
    ahead = lax.broadcasted_iota(jnp.int32, (rows, chunk), 1) - lax.broadcasted_iota(
        jnp.int32, (rows, chunk), 0
    )
    for head in range(0, eq_ref.shape[1], HEAD_DIM):
        columns = pl.ds(head, HEAD_DIM)
        made = jnp.dot(cur_ref[mine, :], aq_ref[:, columns], preferred_element_type=F32)
        made = (made + eq_ref[:, columns].astype(F32)) * inverse[mine, :]
        queries = (made * scale).astype(BF16)
        pair = jnp.concatenate([ak_ref[:, columns], av_ref[:, columns]], axis=1)
        totals = jnp.zeros((rows, HEAD_DIM), F32)
        weighted = jnp.zeros((rows, HEAD_DIM), F32)
        for first in range(0, tokens, chunk):
            here = pl.ds(first, chunk)
            made = jnp.dot(cur_ref[here, :], pair, preferred_element_type=F32)
            keys = (made[:, :HEAD_DIM] + of(ek_refs, first)[:, columns].astype(F32)) * inverse[here, :]
            values = (made[:, HEAD_DIM:] + of(ev_refs, first)[:, columns].astype(F32)) * inverse[here, :]
            scores = lax.dot_general(
                queries, keys.astype(BF16), (((1,), (1,)), ((), ())), preferred_element_type=F32
            )
            weights = jnp.exp(jnp.where(ahead <= own * rows - first, scores, -jnp.inf))
            for lane in range(0, chunk, HEAD_DIM):
                totals = totals + weights[:, lane : lane + HEAD_DIM]
            weighted = weighted + jnp.dot(
                weights.astype(BF16), values.astype(BF16), preferred_element_type=F32
            )
        out_ref[:, columns] = (weighted / jnp.sum(totals, axis=-1, keepdims=True)).astype(BF16)


def attend(index, current, gram, size, width, products):
    (ek_one, ev_one, cross_one, ak, av), (ek_two, ev_two, cross_two, eq, aq) = products
    half = current.shape[0] // 2
    rows, columns = eq.shape
    tokens, channels = current.shape
    whole = lambda shape: pl.BlockSpec(shape, lambda i, n: (0, 0))
    step = HEAD_DIM * (HEADS_A_STEP if columns % (HEAD_DIM * HEADS_A_STEP) == 0 else 1)
    head = lambda n: pl.BlockSpec((n, step), lambda i, k: (0, i))
    return pl.pallas_call(
        functools.partial(attend_kernel, width, HEAD_DIM**-0.5, min(CHUNK, tokens // 2)),
        grid_spec=pltpu.PrefetchScalarGridSpec(
            num_scalar_prefetch=1,
            grid=(columns // step,),
            in_specs=[whole(a.shape) for a in (current, gram, size)]
            + [head(rows)]
            + [head(channels)] * 3
            + [head(half)] * 4
            + [whole(cross_one.shape)] * 2,
            out_specs=head(rows),
            scratch_shapes=[pltpu.VMEM((tokens, HEAD_DIM), F32)],
        ),
        out_shape=jax.ShapeDtypeStruct((rows, columns), BF16),
        compiler_params=pltpu.CompilerParams(vmem_limit_bytes=60 * 2**20),
        cost_estimate=pl.CostEstimate(flops=1, bytes_accessed=1, transcendentals=0),
        name="attend",
    )(index.reshape(1).astype(jnp.int32), current, gram, size, eq, aq, ak, av, ek_one, ek_two, ev_one, ev_two, cross_one, cross_two)


def mlp_kernel(count, parts, gates, per_tile, places, *refs):
    pieces, refs = refs[:count], refs[count:]
    up_parts, down_parts, refs = refs[:parts], refs[parts : 2 * parts], refs[2 * parts + gates :]
    outs, (up, down, up_sem, down_sem) = refs[:count], refs[count:]
    loads = ([], [])
    for i in range(parts):
        for kind, part, full, sem in ((0, up_parts[i], up, up_sem), (1, down_parts[i], down, down_sem)):
            rows = part.shape[kind]
            at = pl.ds(pl.multiple_of(places[i] * rows, rows), rows)
            there = full.at[at, :] if kind == 0 else full.at[:, at]
            loads[kind].append(pltpu.make_async_copy(part, there, sem.at[i]))
    for load in loads[0] + loads[1]:
        load.start()
    for load in loads[0]:
        load.wait()
    sub = pieces[0].shape[0]
    for first in range(0, count, per_tile):
        tile = range(first, min(first + per_tile, count))
        rows = jnp.concatenate([pieces[i][...] for i in tile])
        hidden = jax.nn.gelu(
            jnp.dot(rows, up[...], preferred_element_type=F32), approximate=True
        ).astype(BF16)
        if first == 0:
            for load in loads[1]:
                load.wait()
        terms = jnp.dot(hidden, down[...], preferred_element_type=F32).astype(BF16)
        for n, i in enumerate(tile):
            outs[i][...] = terms[n * sub : (n + 1) * sub]


def mlp(pieces, weights, gates=()):
    places, up_parts, down_parts = weights
    count, (sub, width) = len(pieces), pieces[0].shape
    parts, chunk = len(up_parts), up_parts[0].shape[1]
    vmem = pl.BlockSpec(memory_space=pltpu.VMEM)
    anywhere = pl.BlockSpec(memory_space=pl.ANY)
    return pl.pallas_call(
        functools.partial(mlp_kernel, count, parts, len(gates), max(1, 320 // sub)),
        in_specs=[pl.BlockSpec(memory_space=pltpu.SMEM)]
        + [vmem] * count
        + [anywhere] * (2 * parts + len(gates)),
        out_specs=[vmem] * count,
        out_shape=[jax.ShapeDtypeStruct((sub, width), BF16)] * count,
        scratch_shapes=[
            pltpu.VMEM((width, chunk), BF16),
            pltpu.VMEM((chunk, width), BF16),
            pltpu.SemaphoreType.DMA((parts,)),
            pltpu.SemaphoreType.DMA((parts,)),
        ],
        compiler_params=pltpu.CompilerParams(vmem_limit_bytes=60 * 2**20),
        cost_estimate=pl.CostEstimate(flops=1, bytes_accessed=1, transcendentals=0),
        name="mlp",
    )(places, *pieces, *up_parts, *down_parts, *gates)


def per_device(
    latent, w_in, w_query, w_key, w_value, w_attn_out, w_up, w_down, w_final,
    gain_attn, gain_mlp, gain_final,
):
    grid = Grid()
    rows, channels = latent.shape
    width = w_in.shape[1]
    sub = rows // grid.nh
    tokens = rows * grid.ns
    tables = angle_tables(tokens, width)
    start = grid.s * rows + grid.h * sub

    weights = Weights(grid, w_up, w_down)
    first_two = weights.send(0, 0)
    latent_own = lax.dynamic_slice_in_dim(latent, grid.h * sub, sub)
    means = embedding_means(*tables)
    variance = 0.5 - means * means
    both = (w_key, w_value)
    one = embed_products(grid.s, 0, rows, w_in, tables, means, gain_attn, both)
    turn = after(grid.s, first_two + [one[0]])
    second = weights.send(1, turn - grid.s)
    second_swapped = [weights.swapped[kind, 0] for kind in range(2)] + weights.swap(0)
    two = embed_products(turn, 1, rows, w_in, tables, means, gain_attn, both + (w_query,))
    products = (one, two)
    latent_all = gather_rows(
        grid, latent_own.astype(BF16), gates=[one[0]], late_gates=[two[0]]
    )
    turn = after(grid.s, second + second_swapped + [two[0]])
    third = weights.send(2, turn - grid.s)
    third_swapped = weights.swap(1)
    next_row = grid.seq_shift(latent[:1], -1)
    latent_next = lax.dynamic_slice_in_dim(
        jnp.concatenate([latent, next_row]), grid.h * sub + 1, sub
    )
    wide = w_in.astype(F32)
    wide = wide - jnp.mean(wide, axis=-1, keepdims=True)
    gram = jnp.dot(wide, wide.T, precision=lax.Precision.HIGHEST)
    upper = gram.astype(BF16)
    gram = jnp.concatenate([upper, (gram - upper.astype(F32)).astype(BF16)], axis=1)
    position = (start + jnp.arange(sub)) // FINE
    offset = (start + jnp.arange(sub)) % FINE
    embedding = embed(
        *(jnp.take(t, position, axis=0) for t in tables[:2]),
        *(jnp.take(t, offset, axis=0) for t in tables[2:]),
    )

    current = latent_all
    for step_index in range(ITERS):
        attended = attend(turn if step_index == 0 else grid.s, current, gram, variance, width, products)
        own_rows = lax.dynamic_slice_in_dim(current, start, sub)
        stream_in = jnp.dot(own_rows, w_in, preferred_element_type=F32) + embedding
        zero = 0
        if step_index == 0:
            zero = after(grid.s, third + third_swapped + [attended]) - grid.s
            fourth = weights.send(3, zero)
            fourth_swapped = weights.swap(2)
        stream_attn = stream_in + reduce_head(
            grid,
            jnp.dot(attended, w_attn_out, preferred_element_type=F32).astype(BF16),
            zero,
        )
        if step_index == 0:
            zero = after(grid.s, fourth + fourth_swapped) - grid.s
            weights.swap(3)
        pieces = gather_ring(grid, layer_norm(stream_attn, gain_mlp).astype(BF16), zero)
        if step_index == 0:
            parts = weights.parts()
        half = max(pieces)
        terms, gates = {}, ()
        for part in (
            [k for k in sorted(pieces) if abs(k) <= half // 2],
            [k for k in sorted(pieces) if abs(k) > half // 2],
        ):
            others = [grid.core_swap(pieces[k]) for k in part]
            made = mlp(others + [pieces[k] for k in part], parts, gates)
            gates = (made[0],)
            for k, other, mine in zip(part, made, made[len(part) :]):
                terms[k] = mine.astype(F32) + grid.core_swap(other).astype(F32)
        stream_mlp = stream_attn + reduce_ring(grid, terms)
        final = layer_norm(stream_mlp, gain_final).astype(BF16)
        params = jnp.dot(final, w_final, preferred_element_type=F32)
        moved = latent_next * jnp.exp(jnp.tanh(params[:, channels:])) + params[:, :channels]
        if step_index < ITERS - 1:
            current = gather_rows(grid, moved.astype(BF16), latent_all[:16])

    def next_mirrored(s, h):
        there = s * grid.nh + h + 1
        if there == grid.ns * grid.nh:
            return None
        return grid.ns - 1 - there // grid.nh, there % grid.nh

    first = grid.move(moved[-1:], next_mirrored)
    mirrored = grid.move(moved, lambda s, h: (grid.ns - 1 - s, h))
    is_start = (grid.s == grid.ns - 1) & (grid.h == 0)
    first = jnp.where(is_start, latent_all[:1].astype(F32), first)
    block = jnp.concatenate([first, mirrored[:-1]])[::-1]
    blocks = [block] + [grid.group_shift(block, -j) for j in range(1, grid.groups)]
    heads = [((grid.y + j) % grid.groups) * 2 + grid.c for j in range(grid.groups)]
    blocks += [grid.core_swap(block) for block in blocks]
    heads += [head ^ 1 for head in heads]
    return place(blocks, [grid.nh - 1 - head for head in heads], sub)


def solution(mesh):
    in_specs = (
        P("seq", None),
        P(),
        P(None, "head"),
        P(None, "head"),
        P(None, "head"),
        P("head", None),
        P("seq", "head"),
        P("head", "seq"),
        P(),
        P(),
        P(),
        P(),
    )
    return jax.shard_map(
        per_device, mesh=mesh, in_specs=in_specs, out_specs=P("seq", None), check_vma=False
    )
```

```python
import functools

import jax
import jax.numpy as jnp
from jax import lax
from jax.experimental import pallas as pl
from jax.experimental.pallas import tpu as pltpu
from jax.sharding import PartitionSpec as P

HEAD_DIM = 128
ITERS = 2
EPSILON = 1e-05
FINE = 64
BLOCKS = 2
STRIP = 256
CHUNK = 1024
HEADS_A_STEP = 2
BF16, F32 = jnp.bfloat16, jnp.float32


def layer_norm(stream, gain):
    center = stream - jnp.mean(stream, axis=-1, keepdims=True)
    spread = jnp.mean(center * center, axis=-1, keepdims=True)
    return center * lax.rsqrt(spread + EPSILON) * gain


class Grid:
    def __init__(self):
        self.ns, self.nh = lax.axis_size("seq"), lax.axis_size("head")
        self.s, self.h = lax.axis_index("seq"), lax.axis_index("head")
        self.outer, self.groups = self.ns // 2, self.nh // 2
        self.z, self.x = self.s // 2, self.s % 2
        self.y, self.c = self.h // 2, self.h % 2
        self.ring = []
        for y in range(self.groups):
            line = [(z, y) for z in range(self.outer)]
            self.ring += line if y % 2 == 0 else line[::-1]
        self.place = {zy: i for i, zy in enumerate(self.ring)}

    def move(self, value, target):
        route = []
        for s in range(self.ns):
            for h in range(self.nh):
                there = target(s, h)
                if there is not None:
                    route.append((s * self.nh + h, there[0] * self.nh + there[1]))
        return lax.ppermute(value, ("seq", "head"), route)

    def ring_step(self, value, step):
        def target(s, h):
            i = self.place[(s // 2, h // 2)]
            z, y = self.ring[(i + step) % len(self.ring)]
            return z * 2 + s % 2, y * 2 + h % 2

        return self.move(value, target)

    def seq_shift(self, value, step):
        return self.move(value, lambda s, h: ((s + step) % self.ns, h))

    def outer_shift(self, value, step):
        return self.move(value, lambda s, h: ((s + 2 * step) % self.ns, h))

    def pair_swap(self, value):
        return self.move(value, lambda s, h: (s ^ 1, h))

    def group_shift(self, value, step):
        return self.move(value, lambda s, h: (s, (h + 2 * step) % self.nh))

    def core_swap(self, value):
        return self.move(value, lambda s, h: (s, h ^ 1))


def after_kernel(value_ref, *refs):
    refs[-1][0] = value_ref[0]


def after(value, arrays):
    smem = pl.BlockSpec(memory_space=pltpu.SMEM)
    made = pl.pallas_call(
        after_kernel,
        in_specs=[smem] + [pl.BlockSpec(memory_space=pl.ANY)] * len(arrays),
        out_specs=smem,
        out_shape=jax.ShapeDtypeStruct((1,), jnp.int32),
        name="after",
    )(value.reshape(1).astype(jnp.int32), *arrays)
    return made[0]


def place_kernel(count, sub, shifted, dest_ref, *refs):
    parts, out = refs[:count], refs[count + shifted]
    wide = refs[-1] if shifted else out
    n = 0
    for part in parts:
        for first in range(0, part.shape[0], sub):
            there = pl.ds(pl.multiple_of(dest_ref[n] * sub, sub), sub)
            wide[there, :] = part[pl.ds(first, sub), :].astype(wide.dtype)
            n += 1
    if shifted:
        moved = pltpu.roll(wide[...], 1, axis=0)
        top = lax.broadcasted_iota(jnp.int32, moved.shape, 0) == 0
        out[...] = jnp.where(top, refs[count][:1, :].astype(F32), moved).astype(out.dtype)


def place(parts, dests, sub, first=None):
    width, total = parts[0].shape[1], sum(p.shape[0] for p in parts)
    vmem = pl.BlockSpec(memory_space=pltpu.VMEM)
    extra = [] if first is None else [first]
    return pl.pallas_call(
        functools.partial(place_kernel, len(parts), sub, len(extra)),
        in_specs=[pl.BlockSpec(memory_space=pltpu.SMEM)] + [vmem] * (len(parts) + len(extra)),
        out_specs=vmem,
        out_shape=jax.ShapeDtypeStruct((total, width), parts[0].dtype),
        scratch_shapes=[pltpu.VMEM((total, width), F32)] if extra else [],
        name="place",
    )(jnp.stack(dests).astype(jnp.int32), *parts, *extra)


def gather_seq(grid, own):
    return [own] + [grid.seq_shift(own, -j) for j in range(1, grid.ns)]


def gather_rows(grid, own, first=None, over_seq=None, gates=()):
    sub = own.shape[0]
    over_seq = over_seq or gather_seq(grid, own)
    turn = after(grid.s, gates) if gates else grid.s
    line = place(over_seq, [(turn + j) % grid.ns for j in range(grid.ns)], sub)
    lines = [line] + [grid.group_shift(line, -j) for j in range(1, grid.groups)]
    heads = [((grid.y + j) % grid.groups) * 2 + grid.c for j in range(grid.groups)]
    lines += [grid.core_swap(line) for line in lines]
    heads += [head ^ 1 for head in heads]
    dests = [seq * grid.nh + head for head in heads for seq in range(grid.ns)]
    return place(lines, dests, sub, first)


def gather_ring(grid, own):
    size = len(grid.ring)
    half, cut = size // 2, own.shape[0] // 2
    pieces = {0: own}
    ahead = back = own
    for j in range(1, half):
        ahead, back = grid.ring_step(ahead, 1), grid.ring_step(back, -1)
        pieces[-j], pieces[j] = ahead, back
    pieces[half] = jnp.concatenate(
        [
            grid.ring_step(ahead[:cut], 1),
            grid.ring_step(back[cut:], -1),
        ],
        axis=0,
    )
    return pieces


def reduce_ring(grid, terms):
    size = len(grid.ring)
    half, cut = size // 2, terms[0].shape[0] // 2
    ahead = grid.ring_step(terms[half][:cut].astype(BF16), 1)
    back = grid.ring_step(terms[half][cut:].astype(BF16), -1)
    for j in range(half - 1, 0, -1):
        up, down = terms[j], terms[-j]
        if j == half - 1:
            up = jnp.concatenate([up[:cut] + ahead.astype(F32), up[cut:]], axis=0)
            down = jnp.concatenate([down[:cut], down[cut:] + back.astype(F32)], axis=0)
        else:
            up, down = up + ahead.astype(F32), down + back.astype(F32)
        ahead, back = grid.ring_step(up.astype(BF16), 1), grid.ring_step(down.astype(BF16), -1)
    return terms[0] + ahead.astype(F32) + back.astype(F32)


def reduce_head(grid, term, zero):
    rows, width = term.shape
    blocks = term.reshape(grid.groups, 2, rows // grid.nh, width)
    keep = lax.dynamic_index_in_dim(blocks, grid.c, 1, keepdims=False)
    give = lax.dynamic_index_in_dim(blocks, 1 - grid.c, 1, keepdims=False)
    both = keep.astype(F32) + grid.core_swap(give).astype(F32)
    total = lax.dynamic_index_in_dim(both, grid.y + zero, 0, keepdims=False)
    rounded = both.astype(BF16)
    for j in range(1, grid.groups):
        send = lax.dynamic_index_in_dim(rounded, (grid.y + j) % grid.groups, 0, keepdims=False)
        total = total + grid.group_shift(send, j).astype(F32)
    return total


class Weights:
    def __init__(self, grid, w_up, w_down):
        self.grid, self.w_up, self.w_down = grid, w_up, w_down
        self.chunk, self.rows = w_up.shape[1] // grid.outer, w_up.shape[0]
        self.arrived = {0: self.cut(grid.z)}
        self.swapped = {}

    def partner(self, z, j):
        outer = self.grid.outer
        if j == 0:
            return z
        return z ^ j if outer & (outer - 1) == 0 else (2 * outer + j - z) % outer

    def cut(self, to):
        rows, chunk = self.rows, self.chunk
        up = lax.dynamic_slice_in_dim(self.w_up, to * chunk, chunk, axis=1)
        if chunk % rows:
            down = lax.dynamic_slice_in_dim(self.w_down, to * chunk, chunk).reshape(rows, chunk)
            return jnp.concatenate([up, down], axis=1)
        blocks = [
            lax.dynamic_slice_in_dim(self.w_down, to * chunk + first, rows)
            for first in range(0, chunk, rows)
        ]
        return jnp.concatenate([up] + blocks, axis=1)

    def send(self, j):
        self.arrived[j] = self.grid.move(
            self.cut(self.partner(self.grid.z, j)),
            lambda s, h: (self.partner(s // 2, j) * 2 + s % 2, h),
        )
        return self.arrived[j]

    def swap(self, j):
        self.swapped[j] = self.grid.pair_swap(self.arrived[j])
        return self.swapped[j]

    def parts(self):
        grid, rows, chunk, places, parts = self.grid, self.rows, self.chunk, [], []
        for j in range(grid.outer):
            at = self.partner(grid.z, j) * 2
            places += [at + grid.x, at + 1 - grid.x]
            parts += [self.arrived[j], self.swapped[j]]
        if rows % 128 == 0 and chunk % rows == 0:
            return jnp.stack(places).astype(jnp.int32), parts
        up = jnp.zeros((rows * grid.ns, chunk), BF16)
        down = jnp.zeros((chunk, rows * grid.ns), BF16)
        for at, part in zip(places, parts):
            right = part[:, chunk:]
            if chunk % rows:
                right = right.reshape(chunk, rows)
            else:
                right = jnp.concatenate(
                    [right[:, first : first + rows] for first in range(0, chunk, rows)]
                )
            up = lax.dynamic_update_slice_in_dim(up, part[:, :chunk], at * rows, axis=0)
            down = lax.dynamic_update_slice_in_dim(down, right, at * rows, axis=1)
        return jnp.zeros((1,), jnp.int32), [up, down]


def angle_tables(tokens, width):
    pairs = width // 2
    frequency = jnp.exp(-jnp.log(10000.0) * 2.0 * jnp.arange(pairs).astype(F32) / width)
    coarse = (jnp.arange(tokens // FINE) * FINE).astype(F32)[:, None] * frequency[None, :]
    fine = jnp.arange(FINE).astype(F32)[:, None] * frequency[None, :]
    return jnp.sin(coarse), jnp.cos(coarse), jnp.sin(fine), jnp.cos(fine)


def embedding_means(sin_a, cos_a, sin_b, cos_b):
    left = jnp.concatenate([sin_a, cos_a], axis=1)
    right = jnp.concatenate([cos_b - sin_b, cos_b + sin_b], axis=1)
    total = jnp.dot(left, right.T, precision=lax.Precision.HIGHEST)
    return (total / left.shape[1]).reshape(-1, 1)


def embed(sin_a, cos_a, sin_b, cos_b):
    return jnp.concatenate([sin_a * cos_b + cos_a * sin_b, cos_a * cos_b - sin_a * sin_b], axis=-1)


def embed_kernel(blocks, with_query, ids_ref, *refs):
    w_in_ref, gain_ref, mean_ref, sin_a, cos_a, sin_b, cos_b, wk_ref, wv_ref = refs[:9]
    refs = refs[9:]
    if with_query:
        wq_ref, ek_ref, ev_ref, cross_ref, eq_ref, aq_ref, scaled, plain = refs
    else:
        ek_ref, ev_ref, cross_ref, ak_ref, av_ref, scaled, plain = refs
    step = pl.program_id(0)
    w_in = w_in_ref[...]

    @pl.when(step == 0)
    def _():
        wide = w_in.astype(F32)
        center = wide - jnp.mean(wide, axis=-1, keepdims=True)
        center = (center * gain_ref[...]).astype(BF16)
        pairs = [(wq_ref, aq_ref)] if with_query else [(wk_ref, ak_ref), (wv_ref, av_ref)]
        for weight, out in pairs:
            out[...] = jnp.dot(center, weight[...], preferred_element_type=F32).astype(BF16)

    pairs = sin_b.shape[1]
    for column in range(0, pairs, STRIP):
        low, high = pl.ds(column, STRIP), pl.ds(pairs + column, STRIP)
        for part in range(scaled.shape[0] // FINE):
            sin_coarse, cos_coarse = sin_a[pl.ds(part, 1), low], cos_a[pl.ds(part, 1), low]
            for fine in range(0, FINE, 16):
                rows, thin = pl.ds(part * FINE + fine, 16), pl.ds(fine, 16)
                sin_fine, cos_fine, mean = sin_b[thin, low], cos_b[thin, low], mean_ref[rows, :]
                sines = sin_coarse * cos_fine + cos_coarse * sin_fine - mean
                cosines = cos_coarse * cos_fine - sin_coarse * sin_fine - mean
                scaled[rows, low] = (sines * gain_ref[:, low]).astype(BF16)
                scaled[rows, high] = (cosines * gain_ref[:, high]).astype(BF16)
                plain[rows, low] = sines.astype(BF16)
                plain[rows, high] = cosines.astype(BF16)

    @pl.when(step < blocks)
    def _():
        cross_ref[...] = lax.dot_general(
            plain[...], w_in, (((1,), (1,)), ((), ())), preferred_element_type=F32
        )
        ek_ref[...] = jnp.dot(scaled[...], wk_ref[...], preferred_element_type=F32).astype(BF16)
        ev_ref[...] = jnp.dot(scaled[...], wv_ref[...], preferred_element_type=F32).astype(BF16)

    if with_query:

        @pl.when(step == blocks)
        def _():
            rows = eq_ref.shape[0]
            first = pl.multiple_of(ids_ref[blocks + 1] * rows, rows)
            own = scaled[pl.ds(first, rows), :]
            eq_ref[...] = jnp.dot(own, wq_ref[...], preferred_element_type=F32).astype(BF16)


def embed_products(index, part, rows, w_in, tables, mean, gain, weights):
    sin_a, cos_a, sin_b, cos_b = tables
    channels, width = w_in.shape
    columns = weights[0].shape[1]
    tokens = sin_a.shape[0] * FINE
    block = rows * BLOCKS if tokens % (2 * rows * BLOCKS) == 0 else rows
    coarse, count = block // FINE, tokens // block // 2
    with_query = len(weights) == 3
    sin_a, cos_a = (t.reshape(2 * count, coarse, width // 2) for t in (sin_a, cos_a))
    ids = [part * count + i for i in range(count)]
    ids += [index // (block // rows), index % (block // rows)]
    ids = jnp.stack([jnp.asarray(i, jnp.int32) for i in ids])

    def whole(shape):
        return pl.BlockSpec(
            shape, lambda i, ids: (0,) * len(shape), pipeline_mode=pl.Buffered(buffer_count=1)
        )

    fixed = lambda shape: pl.BlockSpec(shape, lambda i, ids: (0, 0))
    coarse_spec = pl.BlockSpec((None, coarse, width // 2), lambda i, ids: (ids[i], 0, 0))
    token_in = pl.BlockSpec((block, 1), lambda i, ids: (ids[i], 0))
    token = lambda n: pl.BlockSpec((block, n), lambda i, ids: (jnp.minimum(i, count - 1), 0))
    struct = jax.ShapeDtypeStruct
    half = tokens // 2
    small = struct((channels, columns), BF16)
    return pl.pallas_call(
        functools.partial(embed_kernel, count, with_query),
        grid_spec=pltpu.PrefetchScalarGridSpec(
            num_scalar_prefetch=1,
            grid=(count + with_query,),
            in_specs=[
                whole(w_in.shape),
                whole((1, width)),
                token_in,
                coarse_spec,
                coarse_spec,
                whole(sin_b.shape),
                whole(cos_b.shape),
            ]
            + [whole(w.shape) for w in weights],
            out_specs=[token(columns), token(columns), token(channels)]
            + [fixed((rows if with_query else channels, columns)), fixed((channels, columns))],
            scratch_shapes=[pltpu.VMEM((block, width), BF16), pltpu.VMEM((block, width), BF16)],
        ),
        out_shape=[
            struct((half, columns), BF16),
            struct((half, columns), BF16),
            struct((half, channels), F32),
            struct((rows, columns), BF16) if with_query else small,
            small,
        ],
        compiler_params=pltpu.CompilerParams(vmem_limit_bytes=60 * 2**20),
        cost_estimate=pl.CostEstimate(
            flops=8 * tokens * width * columns,
            bytes_accessed=6 * width * columns,
            transcendentals=0,
        ),
        name="embed_products",
    )(ids, w_in, gain.reshape(1, width), mean, sin_a, cos_a, sin_b, cos_b, *weights)


def attend_kernel(
    width, scale, chunk, index_ref, cur_ref, gram_ref, size_ref, eq_ref, aq_ref, ak_ref, av_ref,
    ek_one, ek_two, ev_one, ev_two, cross_one, cross_two, out_ref, inverse,
):
    own = index_ref[0]
    rows, tokens = eq_ref.shape[0], cur_ref.shape[0]
    channels = cur_ref.shape[1]

    def of(refs, first):
        ref, start = refs[first >= tokens // 2], first % (tokens // 2)
        return ref.at[pl.ds(start, chunk)]

    ek_refs, ev_refs, cross_refs = (ek_one, ek_two), (ev_one, ev_two), (cross_one, cross_two)

    @pl.when(pl.program_id(0) == 0)
    def _():
        for first in range(0, tokens, chunk):
            here = pl.ds(first, chunk)
            both = jnp.dot(cur_ref[here, :], gram_ref[...], preferred_element_type=F32)
            both = both[:, :channels] + both[:, channels:] + 2.0 * of(cross_refs, first)[...]
            spread = jnp.sum(both * cur_ref[here, :].astype(F32), axis=-1, keepdims=True)
            inverse[here, :] = jnp.broadcast_to(
                lax.rsqrt(spread / width + size_ref[here, :] + EPSILON), (chunk, HEAD_DIM)
            )

    mine = pl.ds(pl.multiple_of(own * rows, rows), rows)
    ahead = lax.broadcasted_iota(jnp.int32, (rows, chunk), 1) - lax.broadcasted_iota(
        jnp.int32, (rows, chunk), 0
    )
    for head in range(0, eq_ref.shape[1], HEAD_DIM):
        columns = pl.ds(head, HEAD_DIM)
        made = jnp.dot(cur_ref[mine, :], aq_ref[:, columns], preferred_element_type=F32)
        made = (made + eq_ref[:, columns].astype(F32)) * inverse[mine, :]
        queries = (made * scale).astype(BF16)
        pair = jnp.concatenate([ak_ref[:, columns], av_ref[:, columns]], axis=1)
        totals = jnp.zeros((rows, HEAD_DIM), F32)
        weighted = jnp.zeros((rows, HEAD_DIM), F32)
        for first in range(0, tokens, chunk):
            here = pl.ds(first, chunk)
            made = jnp.dot(cur_ref[here, :], pair, preferred_element_type=F32)
            keys = (made[:, :HEAD_DIM] + of(ek_refs, first)[:, columns].astype(F32)) * inverse[here, :]
            values = (made[:, HEAD_DIM:] + of(ev_refs, first)[:, columns].astype(F32)) * inverse[here, :]
            scores = lax.dot_general(
                queries, keys.astype(BF16), (((1,), (1,)), ((), ())), preferred_element_type=F32
            )
            weights = jnp.exp(jnp.where(ahead <= own * rows - first, scores, -jnp.inf))
            for lane in range(0, chunk, HEAD_DIM):
                totals = totals + weights[:, lane : lane + HEAD_DIM]
            weighted = weighted + jnp.dot(
                weights.astype(BF16), values.astype(BF16), preferred_element_type=F32
            )
        out_ref[:, columns] = (weighted / jnp.sum(totals, axis=-1, keepdims=True)).astype(BF16)


def attend(index, current, gram, size, width, products):
    (ek_one, ev_one, cross_one, ak, av), (ek_two, ev_two, cross_two, eq, aq) = products
    half = current.shape[0] // 2
    rows, columns = eq.shape
    tokens, channels = current.shape
    whole = lambda shape: pl.BlockSpec(shape, lambda i, n: (0, 0))
    step = HEAD_DIM * (HEADS_A_STEP if columns % (HEAD_DIM * HEADS_A_STEP) == 0 else 1)
    head = lambda n: pl.BlockSpec((n, step), lambda i, k: (0, i))
    return pl.pallas_call(
        functools.partial(attend_kernel, width, HEAD_DIM**-0.5, min(CHUNK, tokens // 2)),
        grid_spec=pltpu.PrefetchScalarGridSpec(
            num_scalar_prefetch=1,
            grid=(columns // step,),
            in_specs=[whole(a.shape) for a in (current, gram, size)]
            + [head(rows)]
            + [head(channels)] * 3
            + [head(half)] * 4
            + [whole(cross_one.shape)] * 2,
            out_specs=head(rows),
            scratch_shapes=[pltpu.VMEM((tokens, HEAD_DIM), F32)],
        ),
        out_shape=jax.ShapeDtypeStruct((rows, columns), BF16),
        compiler_params=pltpu.CompilerParams(vmem_limit_bytes=60 * 2**20),
        cost_estimate=pl.CostEstimate(
            flops=16 * rows * tokens * columns,
            bytes_accessed=4 * tokens * columns,
            transcendentals=0,
        ),
        name="attend",
    )(index.reshape(1).astype(jnp.int32), current, gram, size, eq, aq, ak, av, ek_one, ek_two, ev_one, ev_two, cross_one, cross_two)


def mlp_kernel(count, parts, gates, per_tile, places, *refs):
    pieces, refs = refs[:count], refs[count:]
    parts, refs = refs[:parts], refs[parts + gates :]
    outs, (up, down, up_sem, down_sem) = refs[:count], refs[count:]
    width, chunk = up.shape
    ups, downs = [], []
    if parts[0].shape == up.shape:
        ups.append(pltpu.make_async_copy(parts[0], up, up_sem.at[0]))
        downs.append(pltpu.make_async_copy(parts[1], down, down_sem.at[0]))
    else:
        for i, part in enumerate(parts):
            rows = part.shape[0]
            at = pl.ds(pl.multiple_of(places[i] * rows, rows), rows)
            left = part.at[:, pl.ds(0, chunk)]
            ups.append(pltpu.make_async_copy(left, up.at[at, :], up_sem.at[i]))
            for n in range(chunk // rows):
                block = part.at[:, pl.ds(chunk + n * rows, rows)]
                there = down.at[pl.ds(n * rows, rows), at]
                downs.append(pltpu.make_async_copy(block, there, down_sem.at[len(downs)]))
    for load in ups + downs:
        load.start()
    for load in ups:
        load.wait()
    sub = pieces[0].shape[0]
    for first in range(0, count, per_tile):
        tile = range(first, min(first + per_tile, count))
        rows = jnp.concatenate([pieces[i][...] for i in tile])
        hidden = jax.nn.gelu(
            jnp.dot(rows, up[...], preferred_element_type=F32), approximate=True
        ).astype(BF16)
        if first == 0:
            for load in downs:
                load.wait()
        terms = jnp.dot(hidden, down[...], preferred_element_type=F32).astype(BF16)
        for n, i in enumerate(tile):
            outs[i][...] = terms[n * sub : (n + 1) * sub]


def mlp(pieces, weights, gates=()):
    places, parts = weights
    count, (sub, width) = len(pieces), pieces[0].shape
    chunk = parts[0].shape[1] if parts[0].shape[0] == width else parts[0].shape[1] // 2
    vmem = pl.BlockSpec(memory_space=pltpu.VMEM)
    anywhere = pl.BlockSpec(memory_space=pl.ANY)
    return pl.pallas_call(
        functools.partial(mlp_kernel, count, len(parts), len(gates), max(1, 320 // sub)),
        in_specs=[pl.BlockSpec(memory_space=pltpu.SMEM)]
        + [vmem] * count
        + [anywhere] * (len(parts) + len(gates)),
        out_specs=[vmem] * count,
        out_shape=[jax.ShapeDtypeStruct((sub, width), BF16)] * count,
        scratch_shapes=[
            pltpu.VMEM((width, chunk), BF16),
            pltpu.VMEM((chunk, width), BF16),
            pltpu.SemaphoreType.DMA((len(parts),)),
            pltpu.SemaphoreType.DMA((len(parts) * max(1, chunk * len(parts) // width),)),
        ],
        compiler_params=pltpu.CompilerParams(vmem_limit_bytes=60 * 2**20),
        cost_estimate=pl.CostEstimate(
            flops=8 * count * sub * width * chunk,
            bytes_accessed=4 * width * chunk,
            transcendentals=0,
        ),
        name="mlp",
    )(places, *pieces, *parts, *gates)


def per_device(
    latent, w_in, w_query, w_key, w_value, w_attn_out, w_up, w_down, w_final,
    gain_attn, gain_mlp, gain_final,
):
    grid = Grid()
    rows, channels = latent.shape
    width = w_in.shape[1]
    sub = rows // grid.nh
    tokens = rows * grid.ns
    tables = angle_tables(tokens, width)
    start = grid.s * rows + grid.h * sub

    weights = Weights(grid, w_up, w_down)
    own_swap = weights.swap(0)
    arrivals = [weights.send(j) for j in range(1, grid.outer)]
    early = max(1, len(arrivals) * 2 // 3)
    latent_own = lax.dynamic_slice_in_dim(latent, grid.h * sub, sub)
    means = embedding_means(*tables)
    variance = 0.5 - means * means
    both = (w_key, w_value)
    latent_own_rounded = latent_own.astype(BF16)
    over_seq = gather_seq(grid, latent_own_rounded)
    turn = after(grid.s, over_seq)
    one = embed_products(turn, 0, rows, w_in, tables, means, gain_attn, both)
    turn = after(turn, [one[0]])
    two = embed_products(turn, 1, rows, w_in, tables, means, gain_attn, both + (w_query,))
    products = (one, two)
    latent_all = gather_rows(
        grid,
        latent_own_rounded,
        over_seq=over_seq,
        gates=arrivals[:early] + [own_swap, two[0]],
    )
    early_swaps = [weights.swap(j) for j in range(1, early + 1)]
    turn = after(grid.s, arrivals[early:] + early_swaps[:1])
    next_row = grid.seq_shift(latent[:1], -1)
    latent_next = lax.dynamic_slice_in_dim(
        jnp.concatenate([latent, next_row]), grid.h * sub + 1, sub
    )
    wide = w_in.astype(F32)
    wide = wide - jnp.mean(wide, axis=-1, keepdims=True)
    gram = jnp.dot(wide, wide.T, precision=lax.Precision.HIGHEST)
    upper = gram.astype(BF16)
    gram = jnp.concatenate([upper, (gram - upper.astype(F32)).astype(BF16)], axis=1)
    position = (start + jnp.arange(sub)) // FINE
    offset = (start + jnp.arange(sub)) % FINE
    embedding = embed(
        *(jnp.take(t, position, axis=0) for t in tables[:2]),
        *(jnp.take(t, offset, axis=0) for t in tables[2:]),
    )

    current = latent_all
    for step_index in range(ITERS):
        attended = attend(turn if step_index == 0 else grid.s, current, gram, variance, width, products)
        own_rows = lax.dynamic_slice_in_dim(current, start, sub)
        stream_in = jnp.dot(own_rows, w_in, preferred_element_type=F32) + embedding
        zero = 0
        if step_index == 0:
            zero = after(grid.s, early_swaps[1:]) - grid.s
            for j in range(early + 1, grid.outer):
                weights.swap(j)
        stream_attn = stream_in + reduce_head(
            grid,
            jnp.dot(attended, w_attn_out, preferred_element_type=F32).astype(BF16),
            zero,
        )
        pieces = gather_ring(grid, layer_norm(stream_attn, gain_mlp).astype(BF16))
        if step_index == 0:
            parts = weights.parts()
        half = max(pieces)
        terms, gates = {}, ()
        for part in (
            [k for k in sorted(pieces) if abs(k) <= half // 2],
            [k for k in sorted(pieces) if abs(k) > half // 2],
        ):
            others = [grid.core_swap(pieces[k]) for k in part]
            made = mlp(others + [pieces[k] for k in part], parts, gates)
            gates = (made[0],)
            for k, other, mine in zip(part, made, made[len(part) :]):
                terms[k] = mine.astype(F32) + grid.core_swap(other).astype(F32)
        stream_mlp = stream_attn + reduce_ring(grid, terms)
        final = layer_norm(stream_mlp, gain_final).astype(BF16)
        params = jnp.dot(final, w_final, preferred_element_type=F32)
        moved = latent_next * jnp.exp(jnp.tanh(params[:, channels:])) + params[:, :channels]
        if step_index < ITERS - 1:
            current = gather_rows(grid, moved.astype(BF16), latent_all[:16])

    def next_mirrored(s, h):
        there = s * grid.nh + h + 1
        if there == grid.ns * grid.nh:
            return None
        return grid.ns - 1 - there // grid.nh, there % grid.nh

    first = grid.move(moved[-1:], next_mirrored)
    mirrored = grid.move(moved, lambda s, h: (grid.ns - 1 - s, h))
    is_start = (grid.s == grid.ns - 1) & (grid.h == 0)
    first = jnp.where(is_start, latent_all[:1].astype(F32), first)
    block = jnp.concatenate([first, mirrored[:-1]])[::-1]
    blocks = [block] + [grid.group_shift(block, -j) for j in range(1, grid.groups)]
    heads = [((grid.y + j) % grid.groups) * 2 + grid.c for j in range(grid.groups)]
    blocks += [grid.core_swap(block) for block in blocks]
    heads += [head ^ 1 for head in heads]
    return place(blocks, [grid.nh - 1 - head for head in heads], sub)


def solution(mesh):
    in_specs = (
        P("seq", None),
        P(),
        P(None, "head"),
        P(None, "head"),
        P(None, "head"),
        P("head", None),
        P("seq", "head"),
        P("head", "seq"),
        P(),
        P(),
        P(),
        P(),
    )
    return jax.shard_map(
        per_device, mesh=mesh, in_specs=in_specs, out_specs=P("seq", None), check_vma=False
    )
```

```python
import functools

import jax
import jax.numpy as jnp
from jax import lax
from jax.experimental import pallas as pl
from jax.experimental.pallas import tpu as pltpu
from jax.sharding import PartitionSpec as P

HEAD_DIM = 128
ITERS = 2
EPSILON = 1e-05
FINE = 64
BLOCKS = 2
STRIP = 256
CHUNK = 1024
MLP_ROWS = 320
HEADS_A_STEP = 2
BF16, F32 = jnp.bfloat16, jnp.float32


def layer_norm(stream, gain):
    center = stream - jnp.mean(stream, axis=-1, keepdims=True)
    spread = jnp.mean(center * center, axis=-1, keepdims=True)
    return center * lax.rsqrt(spread + EPSILON) * gain


class Grid:
    def __init__(self):
        self.ns, self.nh = lax.axis_size("seq"), lax.axis_size("head")
        self.s, self.h = lax.axis_index("seq"), lax.axis_index("head")
        self.outer, self.groups = self.ns // 2, self.nh // 2
        self.z, self.x = self.s // 2, self.s % 2
        self.y, self.c = self.h // 2, self.h % 2
        self.ring = []
        for y in range(self.groups):
            line = [(z, y) for z in range(self.outer)]
            self.ring += line if y % 2 == 0 else line[::-1]
        self.place = {zy: i for i, zy in enumerate(self.ring)}

    def move(self, value, target):
        route = []
        for s in range(self.ns):
            for h in range(self.nh):
                there = target(s, h)
                if there is not None:
                    route.append((s * self.nh + h, there[0] * self.nh + there[1]))
        return lax.ppermute(value, ("seq", "head"), route)

    def ring_step(self, value, step):
        def target(s, h):
            i = self.place[(s // 2, h // 2)]
            z, y = self.ring[(i + step) % len(self.ring)]
            return z * 2 + s % 2, y * 2 + h % 2

        return self.move(value, target)

    def seq_shift(self, value, step):
        return self.move(value, lambda s, h: ((s + step) % self.ns, h))

    def outer_shift(self, value, step):
        return self.move(value, lambda s, h: ((s + 2 * step) % self.ns, h))

    def pair_swap(self, value):
        return self.move(value, lambda s, h: (s ^ 1, h))

    def group_shift(self, value, step):
        return self.move(value, lambda s, h: (s, (h + 2 * step) % self.nh))

    def core_swap(self, value):
        return self.move(value, lambda s, h: (s, h ^ 1))


def after_kernel(value_ref, *refs):
    refs[-1][0] = value_ref[0]


def after(value, arrays):
    smem = pl.BlockSpec(memory_space=pltpu.SMEM)
    made = pl.pallas_call(
        after_kernel,
        in_specs=[smem] + [pl.BlockSpec(memory_space=pl.ANY)] * len(arrays),
        out_specs=smem,
        out_shape=jax.ShapeDtypeStruct((1,), jnp.int32),
        name="after",
    )(value.reshape(1).astype(jnp.int32), *arrays)
    return made[0]


def place_kernel(count, sub, shifted, dest_ref, *refs):
    parts, out = refs[:count], refs[count + shifted]
    wide = refs[-1] if shifted else out
    n = 0
    for part in parts:
        for first in range(0, part.shape[0], sub):
            there = pl.ds(pl.multiple_of(dest_ref[n] * sub, sub), sub)
            wide[there, :] = part[pl.ds(first, sub), :].astype(wide.dtype)
            n += 1
    if shifted:
        moved = pltpu.roll(wide[...], 1, axis=0)
        top = lax.broadcasted_iota(jnp.int32, moved.shape, 0) == 0
        out[...] = jnp.where(top, refs[count][:1, :].astype(F32), moved).astype(out.dtype)


def place(parts, dests, sub, first=None):
    width, total = parts[0].shape[1], sum(p.shape[0] for p in parts)
    vmem = pl.BlockSpec(memory_space=pltpu.VMEM)
    extra = [] if first is None else [first]
    return pl.pallas_call(
        functools.partial(place_kernel, len(parts), sub, len(extra)),
        in_specs=[pl.BlockSpec(memory_space=pltpu.SMEM)] + [vmem] * (len(parts) + len(extra)),
        out_specs=vmem,
        out_shape=jax.ShapeDtypeStruct((total, width), parts[0].dtype),
        scratch_shapes=[pltpu.VMEM((total, width), F32)] if extra else [],
        name="place",
    )(jnp.stack(dests).astype(jnp.int32), *parts, *extra)


def gather_seq(grid, own):
    return [own] + [grid.seq_shift(own, -j) for j in range(1, grid.ns)]


def gather_rows(grid, own, first=None, over_seq=None, gates=()):
    sub = own.shape[0]
    over_seq = over_seq or gather_seq(grid, own)
    turn = after(grid.s, gates) if gates else grid.s
    line = place(over_seq, [(turn + j) % grid.ns for j in range(grid.ns)], sub)
    lines = [line] + [grid.group_shift(line, -j) for j in range(1, grid.groups)]
    heads = [((grid.y + j) % grid.groups) * 2 + grid.c for j in range(grid.groups)]
    lines += [grid.core_swap(line) for line in lines]
    heads += [head ^ 1 for head in heads]
    dests = [seq * grid.nh + head for head in heads for seq in range(grid.ns)]
    return place(lines, dests, sub, first)


def gather_ring(grid, own):
    size = len(grid.ring)
    half, cut = size // 2, own.shape[0] // 2
    pieces = {0: own}
    ahead = back = own
    for j in range(1, half):
        ahead, back = grid.ring_step(ahead, 1), grid.ring_step(back, -1)
        pieces[-j], pieces[j] = ahead, back
    swapped = {j: grid.core_swap(pieces[j]) for j in range(-half // 2, half // 2 + 1) if abs(j) < half - 2}
    zero = after(grid.s, list(swapped.values())) - grid.s
    pieces[half] = jnp.concatenate(
        [
            grid.ring_step(lax.dynamic_slice_in_dim(ahead, zero, cut), 1),
            grid.ring_step(lax.dynamic_slice_in_dim(back, zero + cut, cut), -1),
        ],
        axis=0,
    )
    return pieces, swapped


def reduce_ring(grid, terms):
    size = len(grid.ring)
    half, cut = size // 2, terms[0].shape[0] // 2
    ahead = grid.ring_step(terms[half][:cut].astype(BF16), 1)
    back = grid.ring_step(terms[half][cut:].astype(BF16), -1)
    for j in range(half - 1, 0, -1):
        up, down = terms[j], terms[-j]
        if j == half - 1:
            up = jnp.concatenate([up[:cut] + ahead.astype(F32), up[cut:]], axis=0)
            down = jnp.concatenate([down[:cut], down[cut:] + back.astype(F32)], axis=0)
        else:
            up, down = up + ahead.astype(F32), down + back.astype(F32)
        ahead, back = grid.ring_step(up.astype(BF16), 1), grid.ring_step(down.astype(BF16), -1)
    return terms[0] + ahead.astype(F32) + back.astype(F32)


def reduce_head(grid, term, zero):
    rows, width = term.shape
    blocks = term.reshape(grid.groups, 2, rows // grid.nh, width)
    keep = lax.dynamic_index_in_dim(blocks, grid.c, 1, keepdims=False)
    give = lax.dynamic_index_in_dim(blocks, 1 - grid.c, 1, keepdims=False)
    both = keep.astype(F32) + grid.core_swap(give).astype(F32)
    total = lax.dynamic_index_in_dim(both, grid.y + zero, 0, keepdims=False)
    rounded = both.astype(BF16)
    for j in range(1, grid.groups):
        send = lax.dynamic_index_in_dim(rounded, (grid.y + j) % grid.groups, 0, keepdims=False)
        total = total + grid.group_shift(send, j).astype(F32)
    return total


class Weights:
    def __init__(self, grid, w_up, w_down):
        self.grid, self.w_up, self.w_down = grid, w_up, w_down
        self.chunk, self.rows = w_up.shape[1] // grid.outer, w_up.shape[0]
        self.arrived = {0: self.cut(grid.z)}
        self.swapped = {}

    def partner(self, z, j):
        outer = self.grid.outer
        if j == 0:
            return z
        return z ^ j if outer & (outer - 1) == 0 else (2 * outer + j - z) % outer

    def cut(self, to):
        rows, chunk = self.rows, self.chunk
        up = lax.dynamic_slice_in_dim(self.w_up, to * chunk, chunk, axis=1)
        if chunk % rows:
            down = lax.dynamic_slice_in_dim(self.w_down, to * chunk, chunk).reshape(rows, chunk)
            return jnp.concatenate([up, down], axis=1)
        blocks = [
            lax.dynamic_slice_in_dim(self.w_down, to * chunk + first, rows)
            for first in range(0, chunk, rows)
        ]
        return jnp.concatenate([up] + blocks, axis=1)

    def send(self, j):
        self.arrived[j] = self.grid.move(
            self.cut(self.partner(self.grid.z, j)),
            lambda s, h: (self.partner(s // 2, j) * 2 + s % 2, h),
        )
        return self.arrived[j]

    def swap(self, j):
        self.swapped[j] = self.grid.pair_swap(self.arrived[j])
        return self.swapped[j]

    def parts(self):
        grid, rows, chunk, places, parts = self.grid, self.rows, self.chunk, [], []
        for j in range(grid.outer):
            at = self.partner(grid.z, j) * 2
            places += [at + grid.x, at + 1 - grid.x]
            parts += [self.arrived[j], self.swapped[j]]
        if rows % 128 == 0 and chunk % rows == 0:
            return jnp.stack(places).astype(jnp.int32), parts
        up = jnp.zeros((rows * grid.ns, chunk), BF16)
        down = jnp.zeros((chunk, rows * grid.ns), BF16)
        for at, part in zip(places, parts):
            right = part[:, chunk:]
            if chunk % rows:
                right = right.reshape(chunk, rows)
            else:
                right = jnp.concatenate(
                    [right[:, first : first + rows] for first in range(0, chunk, rows)]
                )
            up = lax.dynamic_update_slice_in_dim(up, part[:, :chunk], at * rows, axis=0)
            down = lax.dynamic_update_slice_in_dim(down, right, at * rows, axis=1)
        return jnp.zeros((1,), jnp.int32), [up, down]


def angle_tables(tokens, width):
    pairs = width // 2
    frequency = jnp.exp(-jnp.log(10000.0) * 2.0 * jnp.arange(pairs).astype(F32) / width)
    coarse = (jnp.arange(tokens // FINE) * FINE).astype(F32)[:, None] * frequency[None, :]
    fine = jnp.arange(FINE).astype(F32)[:, None] * frequency[None, :]
    return jnp.sin(coarse), jnp.cos(coarse), jnp.sin(fine), jnp.cos(fine)


def embedding_means(sin_a, cos_a, sin_b, cos_b):
    left = jnp.concatenate([sin_a, cos_a], axis=1)
    right = jnp.concatenate([cos_b - sin_b, cos_b + sin_b], axis=1)
    total = jnp.dot(left, right.T, precision=lax.Precision.HIGHEST)
    return (total / left.shape[1]).reshape(-1, 1)


def embed(sin_a, cos_a, sin_b, cos_b):
    return jnp.concatenate([sin_a * cos_b + cos_a * sin_b, cos_a * cos_b - sin_a * sin_b], axis=-1)


def embed_kernel(blocks, with_query, ids_ref, *refs):
    w_in_ref, gain_ref, mean_ref, sin_a, cos_a, sin_b, cos_b, wk_ref, wv_ref = refs[:9]
    refs = refs[9:]
    if with_query:
        wq_ref, ek_ref, ev_ref, cross_ref, eq_ref, aq_ref, scaled, plain = refs
    else:
        ek_ref, ev_ref, cross_ref, ak_ref, av_ref, scaled, plain = refs
    step = pl.program_id(0)
    w_in = w_in_ref[...]

    @pl.when(step == 0)
    def _():
        wide = w_in.astype(F32)
        center = wide - jnp.mean(wide, axis=-1, keepdims=True)
        center = (center * gain_ref[...]).astype(BF16)
        pairs = [(wq_ref, aq_ref)] if with_query else [(wk_ref, ak_ref), (wv_ref, av_ref)]
        for weight, out in pairs:
            out[...] = jnp.dot(center, weight[...], preferred_element_type=F32).astype(BF16)

    pairs = sin_b.shape[1]
    for column in range(0, pairs, STRIP):
        low, high = pl.ds(column, STRIP), pl.ds(pairs + column, STRIP)
        for part in range(scaled.shape[0] // FINE):
            sin_coarse, cos_coarse = sin_a[pl.ds(part, 1), low], cos_a[pl.ds(part, 1), low]
            for fine in range(0, FINE, 16):
                rows, thin = pl.ds(part * FINE + fine, 16), pl.ds(fine, 16)
                sin_fine, cos_fine, mean = sin_b[thin, low], cos_b[thin, low], mean_ref[rows, :]
                sines = sin_coarse * cos_fine + cos_coarse * sin_fine - mean
                cosines = cos_coarse * cos_fine - sin_coarse * sin_fine - mean
                scaled[rows, low] = (sines * gain_ref[:, low]).astype(BF16)
                scaled[rows, high] = (cosines * gain_ref[:, high]).astype(BF16)
                plain[rows, low] = sines.astype(BF16)
                plain[rows, high] = cosines.astype(BF16)

    @pl.when(step < blocks)
    def _():
        cross_ref[...] = lax.dot_general(
            plain[...], w_in, (((1,), (1,)), ((), ())), preferred_element_type=F32
        )
        ek_ref[...] = jnp.dot(scaled[...], wk_ref[...], preferred_element_type=F32).astype(BF16)
        ev_ref[...] = jnp.dot(scaled[...], wv_ref[...], preferred_element_type=F32).astype(BF16)

    if with_query:

        @pl.when(step == blocks)
        def _():
            rows = eq_ref.shape[0]
            first = pl.multiple_of(ids_ref[blocks + 1] * rows, rows)
            own = scaled[pl.ds(first, rows), :]
            eq_ref[...] = jnp.dot(own, wq_ref[...], preferred_element_type=F32).astype(BF16)


def embed_products(index, part, rows, w_in, tables, mean, gain, weights):
    sin_a, cos_a, sin_b, cos_b = tables
    channels, width = w_in.shape
    columns = weights[0].shape[1]
    tokens = sin_a.shape[0] * FINE
    block = rows * BLOCKS if tokens % (2 * rows * BLOCKS) == 0 else rows
    coarse, count = block // FINE, tokens // block // 2
    with_query = len(weights) == 3
    sin_a, cos_a = (t.reshape(2 * count, coarse, width // 2) for t in (sin_a, cos_a))
    ids = [part * count + i for i in range(count)]
    ids += [index // (block // rows), index % (block // rows)]
    ids = jnp.stack([jnp.asarray(i, jnp.int32) for i in ids])

    def whole(shape):
        return pl.BlockSpec(
            shape, lambda i, ids: (0,) * len(shape), pipeline_mode=pl.Buffered(buffer_count=1)
        )

    fixed = lambda shape: pl.BlockSpec(shape, lambda i, ids: (0, 0))
    coarse_spec = pl.BlockSpec((None, coarse, width // 2), lambda i, ids: (ids[i], 0, 0))
    token_in = pl.BlockSpec((block, 1), lambda i, ids: (ids[i], 0))
    token = lambda n: pl.BlockSpec((block, n), lambda i, ids: (jnp.minimum(i, count - 1), 0))
    struct = jax.ShapeDtypeStruct
    half = tokens // 2
    small = struct((channels, columns), BF16)
    return pl.pallas_call(
        functools.partial(embed_kernel, count, with_query),
        grid_spec=pltpu.PrefetchScalarGridSpec(
            num_scalar_prefetch=1,
            grid=(count + with_query,),
            in_specs=[
                whole(w_in.shape),
                whole((1, width)),
                token_in,
                coarse_spec,
                coarse_spec,
                whole(sin_b.shape),
                whole(cos_b.shape),
            ]
            + [whole(w.shape) for w in weights],
            out_specs=[token(columns), token(columns), token(channels)]
            + [fixed((rows if with_query else channels, columns)), fixed((channels, columns))],
            scratch_shapes=[pltpu.VMEM((block, width), BF16), pltpu.VMEM((block, width), BF16)],
        ),
        out_shape=[
            struct((half, columns), BF16),
            struct((half, columns), BF16),
            struct((half, channels), F32),
            struct((rows, columns), BF16) if with_query else small,
            small,
        ],
        compiler_params=pltpu.CompilerParams(vmem_limit_bytes=60 * 2**20),
        cost_estimate=pl.CostEstimate(
            flops=8 * tokens * width * columns,
            bytes_accessed=6 * width * columns,
            transcendentals=0,
        ),
        name="embed_products",
    )(ids, w_in, gain.reshape(1, width), mean, sin_a, cos_a, sin_b, cos_b, *weights)


def attend_kernel(
    width, scale, chunk, index_ref, cur_ref, gram_ref, size_ref, eq_ref, aq_ref, ak_ref, av_ref,
    ek_one, ek_two, ev_one, ev_two, cross_one, cross_two, out_ref, inverse,
):
    own = index_ref[0]
    rows, tokens = eq_ref.shape[0], cur_ref.shape[0]
    channels = cur_ref.shape[1]

    def of(refs, first):
        ref, start = refs[first >= tokens // 2], first % (tokens // 2)
        return ref.at[pl.ds(start, chunk)]

    ek_refs, ev_refs, cross_refs = (ek_one, ek_two), (ev_one, ev_two), (cross_one, cross_two)

    @pl.when(pl.program_id(0) == 0)
    def _():
        for first in range(0, tokens, chunk):
            here = pl.ds(first, chunk)
            both = jnp.dot(cur_ref[here, :], gram_ref[...], preferred_element_type=F32)
            both = both[:, :channels] + both[:, channels:] + 2.0 * of(cross_refs, first)[...]
            spread = jnp.sum(both * cur_ref[here, :].astype(F32), axis=-1, keepdims=True)
            inverse[here, :] = jnp.broadcast_to(
                lax.rsqrt(spread / width + size_ref[here, :] + EPSILON), (chunk, HEAD_DIM)
            )

    mine = pl.ds(pl.multiple_of(own * rows, rows), rows)
    ahead = lax.broadcasted_iota(jnp.int32, (rows, chunk), 1) - lax.broadcasted_iota(
        jnp.int32, (rows, chunk), 0
    )
    for head in range(0, eq_ref.shape[1], HEAD_DIM):
        columns = pl.ds(head, HEAD_DIM)
        made = jnp.dot(cur_ref[mine, :], aq_ref[:, columns], preferred_element_type=F32)
        made = (made + eq_ref[:, columns].astype(F32)) * inverse[mine, :]
        queries = (made * scale).astype(BF16)
        pair = jnp.concatenate([ak_ref[:, columns], av_ref[:, columns]], axis=1)
        totals = jnp.zeros((rows, HEAD_DIM), F32)
        weighted = jnp.zeros((rows, HEAD_DIM), F32)
        for first in range(0, tokens, chunk):
            here = pl.ds(first, chunk)
            made = jnp.dot(cur_ref[here, :], pair, preferred_element_type=F32)
            keys = (made[:, :HEAD_DIM] + of(ek_refs, first)[:, columns].astype(F32)) * inverse[here, :]
            values = (made[:, HEAD_DIM:] + of(ev_refs, first)[:, columns].astype(F32)) * inverse[here, :]
            scores = lax.dot_general(
                queries, keys.astype(BF16), (((1,), (1,)), ((), ())), preferred_element_type=F32
            )
            weights = jnp.exp(jnp.where(ahead <= own * rows - first, scores, -jnp.inf))
            for lane in range(0, chunk, HEAD_DIM):
                totals = totals + weights[:, lane : lane + HEAD_DIM]
            weighted = weighted + jnp.dot(
                weights.astype(BF16), values.astype(BF16), preferred_element_type=F32
            )
        out_ref[:, columns] = (weighted / jnp.sum(totals, axis=-1, keepdims=True)).astype(BF16)


def attend(index, current, gram, size, width, products):
    (ek_one, ev_one, cross_one, ak, av), (ek_two, ev_two, cross_two, eq, aq) = products
    half = current.shape[0] // 2
    rows, columns = eq.shape
    tokens, channels = current.shape
    whole = lambda shape: pl.BlockSpec(shape, lambda i, n: (0, 0))
    step = HEAD_DIM * (HEADS_A_STEP if columns % (HEAD_DIM * HEADS_A_STEP) == 0 else 1)
    head = lambda n: pl.BlockSpec((n, step), lambda i, k: (0, i))
    return pl.pallas_call(
        functools.partial(attend_kernel, width, HEAD_DIM**-0.5, min(CHUNK, tokens // 2)),
        grid_spec=pltpu.PrefetchScalarGridSpec(
            num_scalar_prefetch=1,
            grid=(columns // step,),
            in_specs=[whole(a.shape) for a in (current, gram, size)]
            + [head(rows)]
            + [head(channels)] * 3
            + [head(half)] * 4
            + [whole(cross_one.shape)] * 2,
            out_specs=head(rows),
            scratch_shapes=[pltpu.VMEM((tokens, HEAD_DIM), F32)],
        ),
        out_shape=jax.ShapeDtypeStruct((rows, columns), BF16),
        compiler_params=pltpu.CompilerParams(vmem_limit_bytes=60 * 2**20),
        cost_estimate=pl.CostEstimate(
            flops=16 * rows * tokens * columns,
            bytes_accessed=4 * tokens * columns,
            transcendentals=0,
        ),
        name="attend",
    )(index.reshape(1).astype(jnp.int32), current, gram, size, eq, aq, ak, av, ek_one, ek_two, ev_one, ev_two, cross_one, cross_two)


def mlp_kernel(count, parts, per_tile, places, *refs):
    pieces, refs = refs[:count], refs[count:]
    parts, refs = refs[:parts], refs[parts:]
    outs, (up, down, up_sem, down_sem) = refs[:count], refs[count:]
    width, chunk = up.shape
    ups, downs = [], []
    if parts[0].shape == up.shape:
        ups.append(pltpu.make_async_copy(parts[0], up, up_sem.at[0]))
        downs.append(pltpu.make_async_copy(parts[1], down, down_sem.at[0]))
    else:
        for i, part in enumerate(parts):
            rows = part.shape[0]
            at = pl.ds(pl.multiple_of(places[i] * rows, rows), rows)
            left = part.at[:, pl.ds(0, chunk)]
            ups.append(pltpu.make_async_copy(left, up.at[at, :], up_sem.at[i]))
            for n in range(chunk // rows):
                block = part.at[:, pl.ds(chunk + n * rows, rows)]
                there = down.at[pl.ds(n * rows, rows), at]
                downs.append(pltpu.make_async_copy(block, there, down_sem.at[len(downs)]))
    for load in ups + downs:
        load.start()
    for load in ups:
        load.wait()
    sub = pieces[0].shape[0]
    for first in range(0, count, per_tile):
        tile = range(first, min(first + per_tile, count))
        rows = jnp.concatenate([pieces[i][...] for i in tile])
        hidden = jax.nn.gelu(
            jnp.dot(rows, up[...], preferred_element_type=F32), approximate=True
        ).astype(BF16)
        if first == 0:
            for load in downs:
                load.wait()
        terms = jnp.dot(hidden, down[...], preferred_element_type=F32).astype(BF16)
        for n, i in enumerate(tile):
            outs[i][...] = terms[n * sub : (n + 1) * sub]


def mlp(pieces, weights):
    places, parts = weights
    count, (sub, width) = len(pieces), pieces[0].shape
    chunk = parts[0].shape[1] if parts[0].shape[0] == width else parts[0].shape[1] // 2
    vmem = pl.BlockSpec(memory_space=pltpu.VMEM)
    anywhere = pl.BlockSpec(memory_space=pl.ANY)
    return pl.pallas_call(
        functools.partial(mlp_kernel, count, len(parts), max(1, MLP_ROWS // sub)),
        in_specs=[pl.BlockSpec(memory_space=pltpu.SMEM)]
        + [vmem] * count
        + [anywhere] * len(parts),
        out_specs=[vmem] * count,
        out_shape=[jax.ShapeDtypeStruct((sub, width), BF16)] * count,
        scratch_shapes=[
            pltpu.VMEM((width, chunk), BF16),
            pltpu.VMEM((chunk, width), BF16),
            pltpu.SemaphoreType.DMA((len(parts),)),
            pltpu.SemaphoreType.DMA((len(parts) * max(1, chunk * len(parts) // width),)),
        ],
        compiler_params=pltpu.CompilerParams(vmem_limit_bytes=60 * 2**20),
        cost_estimate=pl.CostEstimate(
            flops=8 * count * sub * width * chunk,
            bytes_accessed=4 * width * chunk,
            transcendentals=0,
        ),
        name="mlp",
    )(places, *pieces, *parts)


def per_device(
    latent, w_in, w_query, w_key, w_value, w_attn_out, w_up, w_down, w_final,
    gain_attn, gain_mlp, gain_final,
):
    grid = Grid()
    rows, channels = latent.shape
    width = w_in.shape[1]
    sub = rows // grid.nh
    tokens = rows * grid.ns
    tables = angle_tables(tokens, width)
    start = grid.s * rows + grid.h * sub

    weights = Weights(grid, w_up, w_down)
    own_swap = weights.swap(0)
    arrivals = [weights.send(j) for j in range(1, grid.outer)]
    early = max(1, len(arrivals) * 2 // 3)
    latent_own = lax.dynamic_slice_in_dim(latent, grid.h * sub, sub)
    means = embedding_means(*tables)
    variance = 0.5 - means * means
    both = (w_key, w_value)
    latent_own_rounded = latent_own.astype(BF16)
    over_seq = gather_seq(grid, latent_own_rounded)
    turn = after(grid.s, over_seq)
    one = embed_products(turn, 0, rows, w_in, tables, means, gain_attn, both)
    turn = after(turn, [one[0]])
    two = embed_products(turn, 1, rows, w_in, tables, means, gain_attn, both + (w_query,))
    products = (one, two)
    latent_all = gather_rows(
        grid,
        latent_own_rounded,
        over_seq=over_seq,
        gates=arrivals[:early] + [own_swap, two[0]],
    )
    turn = grid.s
    for j in range(1, early + 1):
        weights.swap(j)
    next_row = grid.seq_shift(latent[:1], -1)
    latent_next = lax.dynamic_slice_in_dim(
        jnp.concatenate([latent, next_row]), grid.h * sub + 1, sub
    )
    wide = w_in.astype(F32)
    wide = wide - jnp.mean(wide, axis=-1, keepdims=True)
    gram = jnp.dot(wide, wide.T, precision=lax.Precision.HIGHEST)
    upper = gram.astype(BF16)
    gram = jnp.concatenate([upper, (gram - upper.astype(F32)).astype(BF16)], axis=1)
    position = (start + jnp.arange(sub)) // FINE
    offset = (start + jnp.arange(sub)) % FINE
    embedding = embed(
        *(jnp.take(t, position, axis=0) for t in tables[:2]),
        *(jnp.take(t, offset, axis=0) for t in tables[2:]),
    )

    current = latent_all
    for step_index in range(ITERS):
        attended = attend(turn if step_index == 0 else grid.s, current, gram, variance, width, products)
        own_rows = lax.dynamic_slice_in_dim(current, start, sub)
        stream_in = jnp.dot(own_rows, w_in, preferred_element_type=F32) + embedding
        zero = 0
        if step_index == 0:
            swaps = [weights.swapped[j] for j in range(1, early + 1)]
            zero = after(grid.s, arrivals[early:] + swaps[:1]) - grid.s
            for j in range(early + 1, grid.outer):
                weights.swap(j)
        stream_attn = stream_in + reduce_head(
            grid,
            jnp.dot(attended, w_attn_out, preferred_element_type=F32).astype(BF16),
            zero,
        )
        pieces, swapped = gather_ring(grid, layer_norm(stream_attn, gain_mlp).astype(BF16))
        if step_index == 0:
            parts = weights.parts()
        order = sorted(pieces)
        others = [swapped.get(k) for k in order]
        others = [grid.core_swap(pieces[k]) if o is None else o for k, o in zip(order, others)]
        made = mlp(others + [pieces[k] for k in order], parts)
        terms = {}
        for k, other, mine in zip(order, made, made[len(order) :]):
            terms[k] = mine.astype(F32) + grid.core_swap(other).astype(F32)
        stream_mlp = stream_attn + reduce_ring(grid, terms)
        final = layer_norm(stream_mlp, gain_final).astype(BF16)
        params = jnp.dot(final, w_final, preferred_element_type=F32)
        moved = latent_next * jnp.exp(jnp.tanh(params[:, channels:])) + params[:, :channels]
        if step_index < ITERS - 1:
            current = gather_rows(grid, moved.astype(BF16), latent_all[:16])

    def next_mirrored(s, h):
        there = s * grid.nh + h + 1
        if there == grid.ns * grid.nh:
            return None
        return grid.ns - 1 - there // grid.nh, there % grid.nh

    first = grid.move(moved[-1:], next_mirrored)
    mirrored = grid.move(moved, lambda s, h: (grid.ns - 1 - s, h))
    is_start = (grid.s == grid.ns - 1) & (grid.h == 0)
    first = jnp.where(is_start, latent_all[:1].astype(F32), first)
    block = jnp.concatenate([first, mirrored[:-1]])[::-1]
    blocks = [block] + [grid.group_shift(block, -j) for j in range(1, grid.groups)]
    heads = [((grid.y + j) % grid.groups) * 2 + grid.c for j in range(grid.groups)]
    blocks += [grid.core_swap(block) for block in blocks]
    heads += [head ^ 1 for head in heads]
    return place(blocks, [grid.nh - 1 - head for head in heads], sub)


def solution(mesh):
    in_specs = (
        P("seq", None),
        P(),
        P(None, "head"),
        P(None, "head"),
        P(None, "head"),
        P("head", None),
        P("seq", "head"),
        P("head", "seq"),
        P(),
        P(),
        P(),
        P(),
    )
    return jax.shard_map(
        per_device, mesh=mesh, in_specs=in_specs, out_specs=P("seq", None), check_vma=False
    )
```

```python
import functools

import jax
import jax.numpy as jnp
from jax import lax
from jax.experimental import pallas as pl
from jax.experimental.pallas import tpu as pltpu
from jax.sharding import PartitionSpec as P

HEAD_DIM = 128
ITERS = 2
EPSILON = 1e-05
FINE = 64
BLOCKS = 2
STRIP = 256
CHUNK = 1024
MLP_ROWS = 320
HEADS_A_STEP = 2
BF16, F32 = jnp.bfloat16, jnp.float32


def layer_norm(stream, gain):
    center = stream - jnp.mean(stream, axis=-1, keepdims=True)
    spread = jnp.mean(center * center, axis=-1, keepdims=True)
    return center * lax.rsqrt(spread + EPSILON) * gain


class Grid:
    def __init__(self):
        self.ns, self.nh = lax.axis_size("seq"), lax.axis_size("head")
        self.s, self.h = lax.axis_index("seq"), lax.axis_index("head")
        self.outer, self.groups = self.ns // 2, self.nh // 2
        self.z, self.x = self.s // 2, self.s % 2
        self.y, self.c = self.h // 2, self.h % 2
        self.ring = []
        for y in range(self.groups):
            line = [(z, y) for z in range(self.outer)]
            self.ring += line if y % 2 == 0 else line[::-1]
        self.place = {zy: i for i, zy in enumerate(self.ring)}

    def move(self, value, target):
        route = []
        for s in range(self.ns):
            for h in range(self.nh):
                there = target(s, h)
                if there is not None:
                    route.append((s * self.nh + h, there[0] * self.nh + there[1]))
        return lax.ppermute(value, ("seq", "head"), route)

    def ring_step(self, value, step):
        def target(s, h):
            i = self.place[(s // 2, h // 2)]
            z, y = self.ring[(i + step) % len(self.ring)]
            return z * 2 + s % 2, y * 2 + h % 2

        return self.move(value, target)

    def seq_shift(self, value, step):
        return self.move(value, lambda s, h: ((s + step) % self.ns, h))

    def outer_shift(self, value, step):
        return self.move(value, lambda s, h: ((s + 2 * step) % self.ns, h))

    def pair_swap(self, value):
        return self.move(value, lambda s, h: (s ^ 1, h))

    def group_shift(self, value, step):
        return self.move(value, lambda s, h: (s, (h + 2 * step) % self.nh))

    def core_swap(self, value):
        return self.move(value, lambda s, h: (s, h ^ 1))


def after_kernel(value_ref, *refs):
    refs[-1][0] = value_ref[0]


def after(value, arrays):
    smem = pl.BlockSpec(memory_space=pltpu.SMEM)
    made = pl.pallas_call(
        after_kernel,
        in_specs=[smem] + [pl.BlockSpec(memory_space=pl.ANY)] * len(arrays),
        out_specs=smem,
        out_shape=jax.ShapeDtypeStruct((1,), jnp.int32),
        name="after",
    )(value.reshape(1).astype(jnp.int32), *arrays)
    return made[0]


def place_kernel(count, sub, shifted, dest_ref, *refs):
    parts, out = refs[:count], refs[count + shifted]
    wide = refs[-1] if shifted else out
    n = 0
    for part in parts:
        for first in range(0, part.shape[0], sub):
            there = pl.ds(pl.multiple_of(dest_ref[n] * sub, sub), sub)
            wide[there, :] = part[pl.ds(first, sub), :].astype(wide.dtype)
            n += 1
    if shifted:
        moved = pltpu.roll(wide[...], 1, axis=0)
        top = lax.broadcasted_iota(jnp.int32, moved.shape, 0) == 0
        out[...] = jnp.where(top, refs[count][:1, :].astype(F32), moved).astype(out.dtype)


def place(parts, dests, sub, first=None):
    width, total = parts[0].shape[1], sum(p.shape[0] for p in parts)
    vmem = pl.BlockSpec(memory_space=pltpu.VMEM)
    extra = [] if first is None else [first]
    return pl.pallas_call(
        functools.partial(place_kernel, len(parts), sub, len(extra)),
        in_specs=[pl.BlockSpec(memory_space=pltpu.SMEM)] + [vmem] * (len(parts) + len(extra)),
        out_specs=vmem,
        out_shape=jax.ShapeDtypeStruct((total, width), parts[0].dtype),
        scratch_shapes=[pltpu.VMEM((total, width), F32)] if extra else [],
        name="place",
    )(jnp.stack(dests).astype(jnp.int32), *parts, *extra)


def gather_seq(grid, own):
    return [own] + [grid.seq_shift(own, -j) for j in range(1, grid.ns)]


def gather_rows(grid, own, first=None, over_seq=None, gates=()):
    sub = own.shape[0]
    over_seq = over_seq or gather_seq(grid, own)
    turn = after(grid.s, gates) if gates else grid.s
    line = place(over_seq, [(turn + j) % grid.ns for j in range(grid.ns)], sub)
    lines = [line] + [grid.group_shift(line, -j) for j in range(1, grid.groups)]
    heads = [((grid.y + j) % grid.groups) * 2 + grid.c for j in range(grid.groups)]
    lines += [grid.core_swap(line) for line in lines]
    heads += [head ^ 1 for head in heads]
    dests = [seq * grid.nh + head for head in heads for seq in range(grid.ns)]
    return place(lines, dests, sub, first)


def gather_ring(grid, own, gates):
    size = len(grid.ring)
    half, cut = size // 2, own.shape[0] // 2
    pieces = {0: own}
    ahead = back = own
    for j in range(1, half):
        ahead, back = grid.ring_step(ahead, 1), grid.ring_step(back, -1)
        pieces[-j], pieces[j] = ahead, back
    swapped = {j: grid.core_swap(pieces[j]) for j in range(-half // 2, half // 2 + 1) if abs(j) < half - 2}
    zero = after(grid.s, list(swapped.values()) + gates) - grid.s
    pieces[half] = jnp.concatenate(
        [
            grid.ring_step(lax.dynamic_slice_in_dim(ahead, zero, cut), 1),
            grid.ring_step(lax.dynamic_slice_in_dim(back, zero + cut, cut), -1),
        ],
        axis=0,
    )
    return pieces, swapped


def reduce_ring(grid, terms):
    size = len(grid.ring)
    half, cut = size // 2, terms[0].shape[0] // 2
    ahead = grid.ring_step(terms[half][:cut].astype(BF16), 1)
    back = grid.ring_step(terms[half][cut:].astype(BF16), -1)
    for j in range(half - 1, 0, -1):
        up, down = terms[j], terms[-j]
        if j == half - 1:
            up = jnp.concatenate([up[:cut] + ahead.astype(F32), up[cut:]], axis=0)
            down = jnp.concatenate([down[:cut], down[cut:] + back.astype(F32)], axis=0)
        else:
            up, down = up + ahead.astype(F32), down + back.astype(F32)
        ahead, back = grid.ring_step(up.astype(BF16), 1), grid.ring_step(down.astype(BF16), -1)
    return terms[0] + ahead.astype(F32) + back.astype(F32)


def reduce_head(grid, term, zero):
    rows, width = term.shape
    blocks = term.reshape(grid.groups, 2, rows // grid.nh, width)
    keep = lax.dynamic_index_in_dim(blocks, grid.c, 1, keepdims=False)
    give = lax.dynamic_index_in_dim(blocks, 1 - grid.c, 1, keepdims=False)
    both = keep.astype(F32) + grid.core_swap(give).astype(F32)
    total = lax.dynamic_index_in_dim(both, grid.y + zero, 0, keepdims=False)
    rounded = both.astype(BF16)
    for j in range(1, grid.groups):
        send = lax.dynamic_index_in_dim(rounded, (grid.y + j) % grid.groups, 0, keepdims=False)
        total = total + grid.group_shift(send, j).astype(F32)
    return total


class Weights:
    def __init__(self, grid, w_up, w_down):
        self.grid, self.w_up, self.w_down = grid, w_up, w_down
        self.chunk, self.rows = w_up.shape[1] // grid.outer, w_up.shape[0]
        self.arrived = {0: self.cut(grid.z)}
        self.swapped = {}

    def partner(self, z, j):
        outer = self.grid.outer
        if j == 0:
            return z
        return z ^ j if outer & (outer - 1) == 0 else (2 * outer + j - z) % outer

    def cut(self, to):
        rows, chunk = self.rows, self.chunk
        up = lax.dynamic_slice_in_dim(self.w_up, to * chunk, chunk, axis=1)
        if chunk % rows:
            down = lax.dynamic_slice_in_dim(self.w_down, to * chunk, chunk).reshape(rows, chunk)
            return jnp.concatenate([up, down], axis=1)
        blocks = [
            lax.dynamic_slice_in_dim(self.w_down, to * chunk + first, rows)
            for first in range(0, chunk, rows)
        ]
        return jnp.concatenate([up] + blocks, axis=1)

    def send(self, j):
        self.arrived[j] = self.grid.move(
            self.cut(self.partner(self.grid.z, j)),
            lambda s, h: (self.partner(s // 2, j) * 2 + s % 2, h),
        )
        return self.arrived[j]

    def swap(self, j):
        self.swapped[j] = self.grid.pair_swap(self.arrived[j])
        return self.swapped[j]

    def parts(self):
        grid, rows, chunk, places, parts = self.grid, self.rows, self.chunk, [], []
        for j in range(grid.outer):
            at = self.partner(grid.z, j) * 2
            places += [at + grid.x, at + 1 - grid.x]
            parts += [self.arrived[j], self.swapped[j]]
        if rows % 128 == 0 and chunk % rows == 0:
            return jnp.stack(places).astype(jnp.int32), parts
        up = jnp.zeros((rows * grid.ns, chunk), BF16)
        down = jnp.zeros((chunk, rows * grid.ns), BF16)
        for at, part in zip(places, parts):
            right = part[:, chunk:]
            if chunk % rows:
                right = right.reshape(chunk, rows)
            else:
                right = jnp.concatenate(
                    [right[:, first : first + rows] for first in range(0, chunk, rows)]
                )
            up = lax.dynamic_update_slice_in_dim(up, part[:, :chunk], at * rows, axis=0)
            down = lax.dynamic_update_slice_in_dim(down, right, at * rows, axis=1)
        return jnp.zeros((1,), jnp.int32), [up, down]


def angle_tables(tokens, width):
    pairs = width // 2
    frequency = jnp.exp(-jnp.log(10000.0) * 2.0 * jnp.arange(pairs).astype(F32) / width)
    coarse = (jnp.arange(tokens // FINE) * FINE).astype(F32)[:, None] * frequency[None, :]
    fine = jnp.arange(FINE).astype(F32)[:, None] * frequency[None, :]
    return jnp.sin(coarse), jnp.cos(coarse), jnp.sin(fine), jnp.cos(fine)


def embedding_means(sin_a, cos_a, sin_b, cos_b):
    left = jnp.concatenate([sin_a, cos_a], axis=1)
    right = jnp.concatenate([cos_b - sin_b, cos_b + sin_b], axis=1)
    total = jnp.dot(left, right.T, precision=lax.Precision.HIGHEST)
    return (total / left.shape[1]).reshape(-1, 1)


def embed(sin_a, cos_a, sin_b, cos_b):
    return jnp.concatenate([sin_a * cos_b + cos_a * sin_b, cos_a * cos_b - sin_a * sin_b], axis=-1)


def embed_kernel(blocks, with_query, ids_ref, *refs):
    w_in_ref, gain_ref, mean_ref, sin_a, cos_a, sin_b, cos_b, wk_ref, wv_ref = refs[:9]
    refs = refs[9:]
    if with_query:
        wq_ref, ek_ref, ev_ref, cross_ref, eq_ref, aq_ref, scaled, plain = refs
    else:
        ek_ref, ev_ref, cross_ref, ak_ref, av_ref, scaled, plain = refs
    step = pl.program_id(0)
    w_in = w_in_ref[...]

    @pl.when(step == 0)
    def _():
        wide = w_in.astype(F32)
        center = wide - jnp.mean(wide, axis=-1, keepdims=True)
        center = (center * gain_ref[...]).astype(BF16)
        pairs = [(wq_ref, aq_ref)] if with_query else [(wk_ref, ak_ref), (wv_ref, av_ref)]
        for weight, out in pairs:
            out[...] = jnp.dot(center, weight[...], preferred_element_type=F32).astype(BF16)

    pairs = sin_b.shape[1]
    for column in range(0, pairs, STRIP):
        low, high = pl.ds(column, STRIP), pl.ds(pairs + column, STRIP)
        for part in range(scaled.shape[0] // FINE):
            sin_coarse, cos_coarse = sin_a[pl.ds(part, 1), low], cos_a[pl.ds(part, 1), low]
            for fine in range(0, FINE, 16):
                rows, thin = pl.ds(part * FINE + fine, 16), pl.ds(fine, 16)
                sin_fine, cos_fine, mean = sin_b[thin, low], cos_b[thin, low], mean_ref[rows, :]
                sines = sin_coarse * cos_fine + cos_coarse * sin_fine - mean
                cosines = cos_coarse * cos_fine - sin_coarse * sin_fine - mean
                scaled[rows, low] = (sines * gain_ref[:, low]).astype(BF16)
                scaled[rows, high] = (cosines * gain_ref[:, high]).astype(BF16)
                plain[rows, low] = sines.astype(BF16)
                plain[rows, high] = cosines.astype(BF16)

    @pl.when(step < blocks)
    def _():
        cross_ref[...] = lax.dot_general(
            plain[...], w_in, (((1,), (1,)), ((), ())), preferred_element_type=F32
        )
        ek_ref[...] = jnp.dot(scaled[...], wk_ref[...], preferred_element_type=F32).astype(BF16)
        ev_ref[...] = jnp.dot(scaled[...], wv_ref[...], preferred_element_type=F32).astype(BF16)

    if with_query:

        @pl.when(step == blocks)
        def _():
            rows = eq_ref.shape[0]
            first = pl.multiple_of(ids_ref[blocks + 1] * rows, rows)
            own = scaled[pl.ds(first, rows), :]
            eq_ref[...] = jnp.dot(own, wq_ref[...], preferred_element_type=F32).astype(BF16)


def embed_products(index, part, rows, w_in, tables, mean, gain, weights):
    sin_a, cos_a, sin_b, cos_b = tables
    channels, width = w_in.shape
    columns = weights[0].shape[1]
    tokens = sin_a.shape[0] * FINE
    block = rows * BLOCKS if tokens % (2 * rows * BLOCKS) == 0 else rows
    coarse, count = block // FINE, tokens // block // 2
    with_query = len(weights) == 3
    sin_a, cos_a = (t.reshape(2 * count, coarse, width // 2) for t in (sin_a, cos_a))
    ids = [part * count + i for i in range(count)]
    ids += [index // (block // rows), index % (block // rows)]
    ids = jnp.stack([jnp.asarray(i, jnp.int32) for i in ids])

    def whole(shape):
        return pl.BlockSpec(
            shape, lambda i, ids: (0,) * len(shape), pipeline_mode=pl.Buffered(buffer_count=1)
        )

    fixed = lambda shape: pl.BlockSpec(shape, lambda i, ids: (0, 0))
    coarse_spec = pl.BlockSpec((None, coarse, width // 2), lambda i, ids: (ids[i], 0, 0))
    token_in = pl.BlockSpec((block, 1), lambda i, ids: (ids[i], 0))
    token = lambda n: pl.BlockSpec((block, n), lambda i, ids: (jnp.minimum(i, count - 1), 0))
    struct = jax.ShapeDtypeStruct
    half = tokens // 2
    small = struct((channels, columns), BF16)
    return pl.pallas_call(
        functools.partial(embed_kernel, count, with_query),
        grid_spec=pltpu.PrefetchScalarGridSpec(
            num_scalar_prefetch=1,
            grid=(count + with_query,),
            in_specs=[
                whole(w_in.shape),
                whole((1, width)),
                token_in,
                coarse_spec,
                coarse_spec,
                whole(sin_b.shape),
                whole(cos_b.shape),
            ]
            + [whole(w.shape) for w in weights],
            out_specs=[token(columns), token(columns), token(channels)]
            + [fixed((rows if with_query else channels, columns)), fixed((channels, columns))],
            scratch_shapes=[pltpu.VMEM((block, width), BF16), pltpu.VMEM((block, width), BF16)],
        ),
        out_shape=[
            struct((half, columns), BF16),
            struct((half, columns), BF16),
            struct((half, channels), F32),
            struct((rows, columns), BF16) if with_query else small,
            small,
        ],
        compiler_params=pltpu.CompilerParams(vmem_limit_bytes=60 * 2**20),
        cost_estimate=pl.CostEstimate(
            flops=8 * tokens * width * columns,
            bytes_accessed=6 * width * columns,
            transcendentals=0,
        ),
        name="embed_products",
    )(ids, w_in, gain.reshape(1, width), mean, sin_a, cos_a, sin_b, cos_b, *weights)


def attend_kernel(
    width, scale, chunk, index_ref, cur_ref, gram_ref, size_ref, eq_ref, aq_ref, ak_ref, av_ref,
    ek_one, ek_two, ev_one, ev_two, cross_one, cross_two, out_ref, inverse,
):
    own = index_ref[0]
    rows, tokens = eq_ref.shape[0], cur_ref.shape[0]
    channels = cur_ref.shape[1]

    def of(refs, first):
        ref, start = refs[first >= tokens // 2], first % (tokens // 2)
        return ref.at[pl.ds(start, chunk)]

    ek_refs, ev_refs, cross_refs = (ek_one, ek_two), (ev_one, ev_two), (cross_one, cross_two)

    @pl.when(pl.program_id(0) == 0)
    def _():
        for first in range(0, tokens, chunk):
            here = pl.ds(first, chunk)
            both = jnp.dot(cur_ref[here, :], gram_ref[...], preferred_element_type=F32)
            both = both[:, :channels] + both[:, channels:] + 2.0 * of(cross_refs, first)[...]
            spread = jnp.sum(both * cur_ref[here, :].astype(F32), axis=-1, keepdims=True)
            inverse[here, :] = jnp.broadcast_to(
                lax.rsqrt(spread / width + size_ref[here, :] + EPSILON), (chunk, HEAD_DIM)
            )

    mine = pl.ds(pl.multiple_of(own * rows, rows), rows)
    ahead = lax.broadcasted_iota(jnp.int32, (rows, chunk), 1) - lax.broadcasted_iota(
        jnp.int32, (rows, chunk), 0
    )
    for head in range(0, eq_ref.shape[1], HEAD_DIM):
        columns = pl.ds(head, HEAD_DIM)
        made = jnp.dot(cur_ref[mine, :], aq_ref[:, columns], preferred_element_type=F32)
        made = (made + eq_ref[:, columns].astype(F32)) * inverse[mine, :]
        queries = (made * scale).astype(BF16)
        pair = jnp.concatenate([ak_ref[:, columns], av_ref[:, columns]], axis=1)
        totals = jnp.zeros((rows, HEAD_DIM), F32)
        weighted = jnp.zeros((rows, HEAD_DIM), F32)
        for first in range(0, tokens, chunk):
            here = pl.ds(first, chunk)
            made = jnp.dot(cur_ref[here, :], pair, preferred_element_type=F32)
            keys = (made[:, :HEAD_DIM] + of(ek_refs, first)[:, columns].astype(F32)) * inverse[here, :]
            values = (made[:, HEAD_DIM:] + of(ev_refs, first)[:, columns].astype(F32)) * inverse[here, :]
            scores = lax.dot_general(
                queries, keys.astype(BF16), (((1,), (1,)), ((), ())), preferred_element_type=F32
            )
            weights = jnp.exp(jnp.where(ahead <= own * rows - first, scores, -jnp.inf))
            for lane in range(0, chunk, HEAD_DIM):
                totals = totals + weights[:, lane : lane + HEAD_DIM]
            weighted = weighted + jnp.dot(
                weights.astype(BF16), values.astype(BF16), preferred_element_type=F32
            )
        out_ref[:, columns] = (weighted / jnp.sum(totals, axis=-1, keepdims=True)).astype(BF16)


def attend(index, current, gram, size, width, products):
    (ek_one, ev_one, cross_one, ak, av), (ek_two, ev_two, cross_two, eq, aq) = products
    half = current.shape[0] // 2
    rows, columns = eq.shape
    tokens, channels = current.shape
    whole = lambda shape: pl.BlockSpec(shape, lambda i, n: (0, 0))
    step = HEAD_DIM * (HEADS_A_STEP if columns % (HEAD_DIM * HEADS_A_STEP) == 0 else 1)
    head = lambda n: pl.BlockSpec((n, step), lambda i, k: (0, i))
    return pl.pallas_call(
        functools.partial(attend_kernel, width, HEAD_DIM**-0.5, min(CHUNK, tokens // 2)),
        grid_spec=pltpu.PrefetchScalarGridSpec(
            num_scalar_prefetch=1,
            grid=(columns // step,),
            in_specs=[whole(a.shape) for a in (current, gram, size)]
            + [head(rows)]
            + [head(channels)] * 3
            + [head(half)] * 4
            + [whole(cross_one.shape)] * 2,
            out_specs=head(rows),
            scratch_shapes=[pltpu.VMEM((tokens, HEAD_DIM), F32)],
        ),
        out_shape=jax.ShapeDtypeStruct((rows, columns), BF16),
        compiler_params=pltpu.CompilerParams(vmem_limit_bytes=60 * 2**20),
        cost_estimate=pl.CostEstimate(
            flops=16 * rows * tokens * columns,
            bytes_accessed=4 * tokens * columns,
            transcendentals=0,
        ),
        name="attend",
    )(index.reshape(1).astype(jnp.int32), current, gram, size, eq, aq, ak, av, ek_one, ek_two, ev_one, ev_two, cross_one, cross_two)


def mlp_kernel(count, parts, per_tile, places, *refs):
    pieces, refs = refs[:count], refs[count:]
    parts, refs = refs[:parts], refs[parts:]
    outs, (up, down, up_sem, down_sem) = refs[:count], refs[count:]
    width, chunk = up.shape
    ups, downs = [], []
    if parts[0].shape == up.shape:
        ups.append(pltpu.make_async_copy(parts[0], up, up_sem.at[0]))
        downs.append(pltpu.make_async_copy(parts[1], down, down_sem.at[0]))
    else:
        for i, part in enumerate(parts):
            rows = part.shape[0]
            at = pl.ds(pl.multiple_of(places[i] * rows, rows), rows)
            left = part.at[:, pl.ds(0, chunk)]
            ups.append(pltpu.make_async_copy(left, up.at[at, :], up_sem.at[i]))
            for n in range(chunk // rows):
                block = part.at[:, pl.ds(chunk + n * rows, rows)]
                there = down.at[pl.ds(n * rows, rows), at]
                downs.append(pltpu.make_async_copy(block, there, down_sem.at[len(downs)]))
    for load in ups + downs:
        load.start()
    for load in ups:
        load.wait()
    sub = pieces[0].shape[0]
    for first in range(0, count, per_tile):
        tile = range(first, min(first + per_tile, count))
        rows = jnp.concatenate([pieces[i][...] for i in tile])
        hidden = jax.nn.gelu(
            jnp.dot(rows, up[...], preferred_element_type=F32), approximate=True
        ).astype(BF16)
        if first == 0:
            for load in downs:
                load.wait()
        terms = jnp.dot(hidden, down[...], preferred_element_type=F32).astype(BF16)
        for n, i in enumerate(tile):
            outs[i][...] = terms[n * sub : (n + 1) * sub]


def mlp(pieces, weights):
    places, parts = weights
    count, (sub, width) = len(pieces), pieces[0].shape
    chunk = parts[0].shape[1] if parts[0].shape[0] == width else parts[0].shape[1] // 2
    vmem = pl.BlockSpec(memory_space=pltpu.VMEM)
    anywhere = pl.BlockSpec(memory_space=pl.ANY)
    return pl.pallas_call(
        functools.partial(mlp_kernel, count, len(parts), max(1, MLP_ROWS // sub)),
        in_specs=[pl.BlockSpec(memory_space=pltpu.SMEM)]
        + [vmem] * count
        + [anywhere] * len(parts),
        out_specs=[vmem] * count,
        out_shape=[jax.ShapeDtypeStruct((sub, width), BF16)] * count,
        scratch_shapes=[
            pltpu.VMEM((width, chunk), BF16),
            pltpu.VMEM((chunk, width), BF16),
            pltpu.SemaphoreType.DMA((len(parts),)),
            pltpu.SemaphoreType.DMA((len(parts) * max(1, chunk * len(parts) // width),)),
        ],
        compiler_params=pltpu.CompilerParams(vmem_limit_bytes=60 * 2**20),
        cost_estimate=pl.CostEstimate(
            flops=8 * count * sub * width * chunk,
            bytes_accessed=4 * width * chunk,
            transcendentals=0,
        ),
        name="mlp",
    )(places, *pieces, *parts)


def per_device(
    latent, w_in, w_query, w_key, w_value, w_attn_out, w_up, w_down, w_final,
    gain_attn, gain_mlp, gain_final,
):
    grid = Grid()
    rows, channels = latent.shape
    width = w_in.shape[1]
    sub = rows // grid.nh
    tokens = rows * grid.ns
    tables = angle_tables(tokens, width)
    start = grid.s * rows + grid.h * sub

    weights = Weights(grid, w_up, w_down)
    own_swap = weights.swap(0)
    arrivals = [weights.send(j) for j in range(1, grid.outer)]
    early = max(1, len(arrivals) * 2 // 3)
    latent_own = lax.dynamic_slice_in_dim(latent, grid.h * sub, sub)
    means = embedding_means(*tables)
    variance = 0.5 - means * means
    both = (w_key, w_value)
    latent_own_rounded = latent_own.astype(BF16)
    over_seq = gather_seq(grid, latent_own_rounded)
    turn = after(grid.s, over_seq)
    one = embed_products(turn, 0, rows, w_in, tables, means, gain_attn, both)
    turn = after(turn, [one[0]])
    two = embed_products(turn, 1, rows, w_in, tables, means, gain_attn, both + (w_query,))
    products = (one, two)
    latent_all = gather_rows(
        grid,
        latent_own_rounded,
        over_seq=over_seq,
        gates=arrivals[:early] + [own_swap, two[0]],
    )
    early_swaps = [weights.swap(j) for j in range(1, early + 1)]
    turn = after(grid.s, early_swaps[:1])
    next_row = grid.seq_shift(latent[:1], -1)
    latent_next = lax.dynamic_slice_in_dim(
        jnp.concatenate([latent, next_row]), grid.h * sub + 1, sub
    )
    wide = w_in.astype(F32)
    wide = wide - jnp.mean(wide, axis=-1, keepdims=True)
    gram = jnp.dot(wide, wide.T, precision=lax.Precision.HIGHEST)
    upper = gram.astype(BF16)
    gram = jnp.concatenate([upper, (gram - upper.astype(F32)).astype(BF16)], axis=1)
    position = (start + jnp.arange(sub)) // FINE
    offset = (start + jnp.arange(sub)) % FINE
    embedding = embed(
        *(jnp.take(t, position, axis=0) for t in tables[:2]),
        *(jnp.take(t, offset, axis=0) for t in tables[2:]),
    )

    current = latent_all
    for step_index in range(ITERS):
        attended = attend(turn if step_index == 0 else grid.s, current, gram, variance, width, products)
        own_rows = lax.dynamic_slice_in_dim(current, start, sub)
        stream_in = jnp.dot(own_rows, w_in, preferred_element_type=F32) + embedding
        zero = 0
        if step_index == 0:
            zero = after(grid.s, arrivals[early:] + early_swaps[1:]) - grid.s
            late_swaps = [weights.swap(j) for j in range(early + 1, grid.outer)]
        stream_attn = stream_in + reduce_head(
            grid,
            jnp.dot(attended, w_attn_out, preferred_element_type=F32).astype(BF16),
            zero,
        )
        pieces, swapped = gather_ring(
            grid,
            layer_norm(stream_attn, gain_mlp).astype(BF16),
            late_swaps if step_index == 0 else [],
        )
        if step_index == 0:
            parts = weights.parts()
        order = sorted(pieces)
        others = [swapped.get(k) for k in order]
        others = [grid.core_swap(pieces[k]) if o is None else o for k, o in zip(order, others)]
        made = mlp(others + [pieces[k] for k in order], parts)
        terms = {}
        for k, other, mine in zip(order, made, made[len(order) :]):
            terms[k] = mine.astype(F32) + grid.core_swap(other).astype(F32)
        stream_mlp = stream_attn + reduce_ring(grid, terms)
        final = layer_norm(stream_mlp, gain_final).astype(BF16)
        params = jnp.dot(final, w_final, preferred_element_type=F32)
        moved = latent_next * jnp.exp(jnp.tanh(params[:, channels:])) + params[:, :channels]
        if step_index < ITERS - 1:
            current = gather_rows(grid, moved.astype(BF16), latent_all[:16])

    def next_mirrored(s, h):
        there = s * grid.nh + h + 1
        if there == grid.ns * grid.nh:
            return None
        return grid.ns - 1 - there // grid.nh, there % grid.nh

    first = grid.move(moved[-1:], next_mirrored)
    mirrored = grid.move(moved, lambda s, h: (grid.ns - 1 - s, h))
    is_start = (grid.s == grid.ns - 1) & (grid.h == 0)
    first = jnp.where(is_start, latent_all[:1].astype(F32), first)
    block = jnp.concatenate([first, mirrored[:-1]])[::-1]
    blocks = [block] + [grid.group_shift(block, -j) for j in range(1, grid.groups)]
    heads = [((grid.y + j) % grid.groups) * 2 + grid.c for j in range(grid.groups)]
    blocks += [grid.core_swap(block) for block in blocks]
    heads += [head ^ 1 for head in heads]
    return place(blocks, [grid.nh - 1 - head for head in heads], sub)


def solution(mesh):
    in_specs = (
        P("seq", None),
        P(),
        P(None, "head"),
        P(None, "head"),
        P(None, "head"),
        P("head", None),
        P("seq", "head"),
        P("head", "seq"),
        P(),
        P(),
        P(),
        P(),
    )
    return jax.shard_map(
        per_device, mesh=mesh, in_specs=in_specs, out_specs=P("seq", None), check_vma=False
    )
```
